128 devices in a mesh: gx: 32 (over y, z_lo, x), gy: 4 (over z_hi, core).
Axes of the slice: x: 4, y: 4, z: 4 (z_hi: 2, z_lo: 2; z = z_hi * 2 + z_lo), core: 2. Of those that a mesh axis runs over, the one named last changes fastest.
Arguments:
- noisy: float32 [16, 512, 512], P(None, 'gx', 'gy'), may hold values from -6 to 6
- strength: float32 [16], replicated, may hold values from 0.5 to 4
Outputs:
- denoised: float32 [16, 512, 512], P(None, 'gx', 'gy')
The draws below stay inside these ranges and needn't reach their ends.
All inputs are finite; a program needn't handle non-finite values.
Results may differ from the reference program's by a relative error of at most 0.00002.
Values sent between devices are 32-bit elements; how exact they have to be, the bound alone decides.
No kernel may reach another device: no remote copies, remote signals or barrier semaphores. Data moves between devices by JAX's collectives and lax.ppermute only.
A program may use at most 128 MiB of HBM per device.

```python
import math
import jax
import jax.numpy as jnp

NZ = 16
NX = 512
NY = 512


def shard_levels(own_key, shape, pieces, least, top_value):
    def one(axis_at, blocks):
        heights = jax.random.uniform(jax.random.fold_in(jax.random.fold_in(own_key, 6), axis_at), (blocks,), jnp.float32, least / len(pieces), top_value / len(pieces))
        return jnp.repeat(jnp.exp(heights), shape[axis_at] // blocks).reshape((-1,) + (1,) * (len(shape) - axis_at - 1))

    factor_of = one(*pieces[0])
    for cut in pieces[1:]:
        factor_of = factor_of * one(*cut)
    return factor_of


def bell_draw(own_key, dims, scale, reach, shards=(), kind=jnp.bfloat16):
    array = scale * jax.random.normal(own_key, dims, jnp.float32)
    if shards:
        array = array * shard_levels(own_key, dims, shards, -0.22, 0.18)
    return jnp.clip(array, -reach, reach).astype(kind)


def setup_inputs(seed: int = 0) -> dict:
    arg_keys = jax.random.split(jax.random.key(seed), 3)
    return {
        "noisy": bell_draw(arg_keys[0], (NZ, NX, NY), 1.0, 6.0, ((1, 32), (2, 4)), jnp.float32),
        "strength": jnp.clip(jnp.exp(jax.random.uniform(arg_keys[1], (NZ,), jnp.float32, math.log(0.5), math.log(4.0))), 0.5, 4.0),
    }


def half_offsets():
    found = []
    for shift_z in range(-2, 3):
        for shift_x in range(-2, 3):
            for shift_y in range(-2, 3):
                if (shift_z, shift_x, shift_y) > (0, 0, 0):
                    found.append((shift_z, shift_x, shift_y))
    return found


def patch_distance(padded, shift_z, shift_x, shift_y, span_z, span_x, span_y):
    base = padded[2:span_z + 6, 2:span_x + 6, 2:span_y + 6]
    moved = padded[2 + shift_z:span_z + 6 + shift_z, 2 + shift_x:span_x + 6 + shift_x, 2 + shift_y:span_y + 6 + shift_y]
    squared = (base - moved) * (base - moved)
    along_z = squared[0:span_z]
    for step in range(1, 5):
        along_z = along_z + squared[step:step + span_z]
    along_x = along_z[:, 0:span_x]
    for step in range(1, 5):
        along_x = along_x + along_z[:, step:step + span_x]
    along_y = along_x[:, :, 0:span_y]
    for step in range(1, 5):
        along_y = along_y + along_x[:, :, step:step + span_y]
    return along_y / 125.0


def reference(noisy, strength):
    span_z, span_x, span_y = noisy.shape
    padded = jnp.pad(noisy, 4)
    inside = jnp.pad(jnp.ones(noisy.shape, jnp.float32), 2)
    scale = strength[:, None, None]
    weighted = noisy
    totals = jnp.ones(noisy.shape, jnp.float32)
    back_weighted = jnp.zeros((span_z + 4, span_x + 4, span_y + 4), jnp.float32)
    back_totals = jnp.zeros((span_z + 4, span_x + 4, span_y + 4), jnp.float32)
    for shift_z, shift_x, shift_y in half_offsets():
        distance = patch_distance(padded, shift_z, shift_x, shift_y, span_z, span_x, span_y)
        valid = inside[2 + shift_z:2 + shift_z + span_z, 2 + shift_x:2 + shift_x + span_x, 2 + shift_y:2 + shift_y + span_y]
        weight = jnp.exp(-distance / scale) * valid
        partner = padded[4 + shift_z:4 + shift_z + span_z, 4 + shift_x:4 + shift_x + span_x, 4 + shift_y:4 + shift_y + span_y]
        weighted = weighted + weight * partner
        totals = totals + weight
        back_weighted = back_weighted.at[2 + shift_z:2 + shift_z + span_z, 2 + shift_x:2 + shift_x + span_x, 2 + shift_y:2 + shift_y + span_y].add(weight * noisy)
        back_totals = back_totals.at[2 + shift_z:2 + shift_z + span_z, 2 + shift_x:2 + shift_x + span_x, 2 + shift_y:2 + shift_y + span_y].add(weight)
    weighted = weighted + back_weighted[2:-2, 2:-2, 2:-2]
    totals = totals + back_totals[2:-2, 2:-2, 2:-2]
    return weighted / totals
```

```python
import math
import jax, jax.numpy as jnp
from jax import lax
from jax.sharding import PartitionSpec as P
from jax.experimental import pallas as pl
from jax.experimental.pallas import tpu as pltpu
F=jnp.float32
B=jnp.bfloat16
def lroll(v,s):
    s%=128
    return v if s==0 else pltpu.roll(v,s,1)
def moved(mm,sy,row,sz,i):
    k=sz+i
    return mm[sy,row,k%2,k//2:k//2+8]
def prepare(nx,n_ref,mm,sq,rows_e,ee):
    zero=jnp.zeros((8,128),F)
    for x in range(nx+8):
        for i in range(2):
            v=n_ref[x,i]
            for sy in range(5):
                mm[sy,x,i,0:8]=lroll(v,2-sy)
                mm[sy,x,i,8:16]=zero
    for sy in range(5):
        for x in range(nx+8):
            for j in range(3): ee[sy,x,j]=zero
    g=(nx+8)//4
    flat=n_ref.reshape((nx+8)*16,128)
    def ym(d): return (d+lroll(d,1))+(lroll(d,2)+lroll(d,127))+lroll(d,126)
    for i in range(2):
        for b in range(-(-(nx+8)//8)):
            c=min(8,nx+8-8*b)
            v=flat[pl.ds(i*8+128*b,c,stride=16)]
            sq[i,8*b:8*b+c]=v*v
    res=[[],[]]
    for i in range(2):
        for b in range(-(-(nx+4)//8)):
            c=min(8,nx+4-8*b)
            t=sq[i,8*b:8*b+c]
            for s in range(1,5): t=t+sq[i,8*b+s:8*b+s+c]
            res[i].append(ym(t))
    ef=ee.reshape(5*(nx+8)*3*8,128)
    for b in range(-(-(nx+4)//8)):
        c=min(8,nx+4-8*b)
        three=(res[0][b],res[0][b]+res[1][b],res[1][b])
        for j in range(3):
            for sy in range(5):
                ef[pl.ds(((sy*(nx+8)+8*b+2)*3+j)*8,c,stride=24)]=lroll(three[j],2-sy)
def sums(nx,sz,sx,sy,n_ref,mm,zs,tb,o,base):
    x0=-max(0,sx); n=nx+abs(sx)
    qc={}; pc={}; cc={}
    def q(m):
        if m not in qc:
            x=x0-2+m
            r=[]
            for i in range(2):
                d=n_ref[x+4,i]-moved(mm,sy,x+sx+4,sz,i)
                r.append(d*d)
            qc[m]=r
        return qc[m]
    def p(m):
        if m not in pc:
            u,v=q(m),q(m+1)
            pc[m]=[u[0]+v[0],u[1]+v[1]]
        return pc[m]
    def common(j):
        if j not in cc:
            u,v=p(j+1),p(j+3)
            cc[j]=[u[0]+v[0],u[1]+v[1]]
        return cc[j]
    for j in range(n):
        if j%2==0: c=common(j); e=q(j)
        else: c=common(j-1); e=q(j+4)
        t=[c[0]+e[0],c[1]+e[1]]
        both=t[0]+t[1]
        zs[o,j,0,8:16]=both
        zs[o,j,1,8:16]=t[0]
        zs[o,j,2,8:16]=t[1]
        d=jnp.concatenate([both+zs[o,j,0,7:15]+zs[o,j,1,9:17], both+zs[o,j,0,9:17]+zs[o,j,2,7:15]],0)
        hi=d.astype(B)
        tb[base+16*j:base+16*j+16,0:128]=hi
        tb[base+16*j:base+16*j+16,128:256]=(d-hi.astype(F)).astype(B)
def weights(nx,sz,sx,sy,r,ee,wb,o,ks,mlo,mhi,ymask):
    x0=-max(0,sx); n=nx+abs(sx)
    for j in range(n):
        x=x0+j
        for i in range(2):
            v=r[16*j+8*i:16*j+8*i+8]
            if sz: v=v+ee[sy,x+sx+4,(sz-1)*(1+i)]
            w=jnp.exp2(v*ks[i])
            if x<0 or x+sx<0: w=w*mlo
            if x>=nx or x+sx>=nx: w=w*mhi
            if ymask is not None: w=w*ymask[sy]
            wb[o,j,i]=w
def offs(sz): return (1,2) if sz==0 else (-2,-1,0,1,2)
def gather(nx,sy,n_ref,mm,wb,index,zg,acc_w,acc_t):
    bot=lax.broadcasted_iota(jnp.int32,(8,128),0)==7
    add=lambda a,b: b if a is None else a+b
    back=jnp.where(sy<2,sy+126,sy-2)
    for x in range(nx):
        fw=[None,None]; ft=[None,None]
        bw=[[None]*2 for _ in range(3)]; bt=[[None]*2 for _ in range(3)]
        for sz in range(3):
            t2=[None,None]
            for sx in (0,)*(sz==0)+offs(sz):
                o=index[sz,sx]; x0=-max(0,sx)
                for i in range(2):
                    w=wb[o,x-x0,i]
                    fw[i]=add(fw[i],w*moved(mm,sy,x+sx+4,sz,i))
                    t2[i]=add(t2[i],w)
                    w=wb[o,x-sx-x0,i]
                    bw[sz][i]=add(bw[sz][i],w*n_ref[x-sx+4,i])
                    bt[sz][i]=add(bt[sz][i],w)
            if sz==2: t2[0]=jnp.where(bot,0.0,t2[0])
            if sz>=1: t2[1]=jnp.where(bot,0.0,t2[1])
            for i in range(2): ft[i]=add(ft[i],t2[i])
        for m,(b,f,acc) in enumerate(((bw,fw,acc_w),(bt,ft,acc_t))):
            zg[x,m,0,8:16]=b[1][1]+b[2][0]
            zg[x,m,1,8:16]=b[2][1]
            even=b[0][0]+zg[x,m,0,7:15]
            odd=b[0][1]+b[1][0]+zg[x,m,1,7:15]
            acc[x,0]=acc[x,0]+f[0]+pltpu.roll(even,back,1)
            acc[x,1]=acc[x,1]+f[1]+pltpu.roll(odd,back,1)
GROUPS=[[(sz,sx) for sx in offs(sz)] for sz in range(3)]
def core(nx,n_ref,sc,ks,mlo,mhi,ymask):
    mm,sq,ee,zs,zg,tb,wb,acc_w,acc_t=sc
    index={}
    for sz in range(3):
        for sx in offs(sz): index[sz,sx]=len(index)
    index[0,0]=len(index)
    zero=jnp.zeros((8,128),F)
    for x in range(nx):
        for i in range(2):
            acc_w[x,i]=n_ref[x+4,i]; acc_t[x,i]=zero+1.0
            wb[index[0,0],x,i]=zero
            for m in range(2):
                zg[x,m,i,0:8]=zero
    for o in range(13):
        for j in range(nx+2):
            for b in range(3):
                zs[o,j,b,0:8]=zero; zs[o,j,b,16:24]=zero
    prepare(nx,n_ref,mm,sq,None,ee)
    r=lax.broadcasted_iota(jnp.int32,(256,128),0)%128
    c=lax.broadcasted_iota(jnp.int32,(256,128),1)
    band=jnp.where(abs(r-c)<=2,1.0,0.0).astype(B)
    def body(sy,_):
        for group in GROUPS:
            base=0; at=[]
            for sz,sx in group:
                sums(nx,sz,sx,sy,n_ref,mm,zs,tb,index[sz,sx],base)
                at.append(base); base+=16*(nx+abs(sx))
            r=jnp.dot(tb[0:base],band,preferred_element_type=F)
            for (sz,sx),p in zip(group,at):
                weights(nx,sz,sx,sy,r[p:p+16*(nx+abs(sx))],ee,wb,index[sz,sx],ks,mlo,mhi,ymask)
        @pl.when(sy>2)
        def _():
            sums(nx,0,0,sy,n_ref,mm,zs,tb,index[0,0],0)
            weights(nx,0,0,sy,jnp.dot(tb[0:16*nx],band,preferred_element_type=F),ee,wb,index[0,0],ks,mlo,mhi,ymask)
        gather(nx,sy,n_ref,mm,wb,index,zg,acc_w,acc_t)
        return 0
    lax.fori_loop(0,5,body,0)
def scratch(nx):
    V=pltpu.VMEM
    return [V((5,nx+8,2,16,128),F),V((2,nx+16,128),F),V((5,nx+8,3,8,128),F),
            V((13,nx+2,3,24,128),F),V((nx,2,2,16,128),F),V((13*16*(nx+2),256),B),V((13,nx+2,2,8,128),F),
            V((nx,2,8,128),F),V((nx,2,8,128),F)]

HALO=4
def lanes(): return lax.broadcasted_iota(jnp.int32,(8,128),1)
def pack_kernel(n_ref,low_ref,high_ref):
    flat=n_ref.reshape(256,128)
    for x in range(HALO):
        for i in range(2):
            low_ref[x,i]=flat[pl.ds(i*16+x,8,stride=32)]
            high_ref[x,i]=flat[pl.ds(i*16+12+x,8,stride=32)]
def rows_kernel(n_ref,low_ref,high_ref,full_ref,rim_ref,left_ref,right_ref,u):
    flat=n_ref.reshape(256,128)
    for x in range(HALO):
        for i in range(2):
            full_ref[x,i]=low_ref[x,i]
            full_ref[20+x,i]=high_ref[x,i]
    for x in range(16):
        for i in range(2):
            full_ref[4+x,i]=flat[pl.ds(i*16+x,8,stride=32)]
    ln=lanes()
    for x in range(24):
        for i in range(2):
            v=full_ref[x,i]
            u[x,i]=jnp.where((ln>=4)&(ln<12),lroll(v,4),jnp.where((ln>=16)&(ln<24),lroll(v,24),0.0))
    for x in range(12):
        for i in range(2):
            rim_ref[x,i]=(u[x,i]+lroll(u[x+4,i],32))+(lroll(u[x+8,i],64)+lroll(u[x+12,i],96))
    slot=(ln%32)//4
    for g in range(3):
        for ref,at in ((left_ref,4),(right_ref,20)):
            m=jnp.zeros((8,128),F)
            for t in range(8):
                m=jnp.where(slot==t,lroll(rim_ref[4*g+t//2,t%2],4*t-at),m)
            ref[g]=m
def main_kernel(s_ref,n_ref,k_ref,o_ref,*sc):
    one=jnp.ones((8,128),F)
    core(16,n_ref,sc,(k_ref[0],k_ref[1]),one*s_ref[0],one*s_ref[1],None)
    for x in range(16):
        for i in range(2): o_ref[x,i]=sc[-2][x,i]/sc[-1][x,i]
def rim_kernel(s_ref,rim_ref,left_ref,right_ref,k_ref,mid_ref,o_ref,r_ref,ym,ro,*sc):
    ln=lanes(); in_strip=ln%32
    for x in range(12):
        g,t=x//4,(x%4)*2
        for i in range(2):
            v=rim_ref[x,i]
            v=jnp.where(in_strip<4,lroll(left_ref[g],-4*(t+i)),v)
            r_ref[x,i]=jnp.where((in_strip>=24)&(in_strip<28),lroll(right_ref[g],24-4*(t+i)),v)
    for sy in range(5):
        bad_left=(in_strip<4)|((in_strip+sy-2<4)&(in_strip<16))
        c=in_strip-16
        bad_right=(c>=8)|((c+sy-2>=8)&(c>=0))
        ym[sy]=jnp.where(bad_left,s_ref[2],1.0)*jnp.where(bad_right,s_ref[3],1.0)
    mlo=jnp.where(ln<32,s_ref[0],1.0)
    mhi=jnp.where(ln>=96,s_ref[1],1.0)
    core(4,r_ref,sc,(k_ref[0],k_ref[1]),mlo,mhi,ym)
    for x in range(4):
        for i in range(2): ro[x,i]=sc[-2][x,i]/sc[-1][x,i]
    flat=o_ref.reshape(256,128)
    for x in range(16):
        k=x//4
        for i in range(2):
            v=ro[x%4,i]
            w=jnp.where(ln<4,lroll(v,-32*k-4),jnp.where(ln>=124,lroll(v,104-32*k),mid_ref[x,i]))
            flat[pl.ds(i*16+x,8,stride=32)]=w
def shape(*dims): return jax.ShapeDtypeStruct(dims,F)
def params(): return pltpu.CompilerParams(vmem_limit_bytes=40*2**20)
def passed_along(value,axis,steps):
    count=lax.axis_size(axis)
    first,last=max(0,-steps),min(count,count-steps)
    return lax.ppermute(value,axis,[(a,a+steps) for a in range(first,last)])
def per_device(noisy,strength):
    gx,gy=lax.axis_index("gx"),lax.axis_index("gy")
    edges=jnp.stack([gx>0,gx<lax.axis_size("gx")-1,gy>0,gy<lax.axis_size("gy")-1]).astype(F)
    rate=(-math.log2(math.e)/125.0)/strength
    rate=jnp.broadcast_to(rate.reshape(8,2).T[:,:,None],(2,8,128))
    smem=pl.BlockSpec(memory_space=pltpu.SMEM)
    vmem=pl.BlockSpec(memory_space=pltpu.VMEM)
    first,last=pl.pallas_call(pack_kernel,out_shape=(shape(4,2,8,128),)*2,name="pack_rows")(noisy)
    below=passed_along(last,"gx",1)
    above=passed_along(first,"gx",-1)
    full,rim,to_left,to_right=pl.pallas_call(rows_kernel,out_shape=(shape(24,2,8,128),shape(12,2,8,128),shape(3,8,128),shape(3,8,128)),
        scratch_shapes=[pltpu.VMEM((24,2,8,128),F)],name="rows")(noisy,below,above)
    left=passed_along(to_right,"gy",1)
    right=passed_along(to_left,"gy",-1)
    mid=pl.pallas_call(main_kernel,out_shape=shape(16,2,8,128),in_specs=[smem,vmem,vmem],scratch_shapes=scratch(16),compiler_params=params(),
        cost_estimate=pl.CostEstimate(flops=80_000_000,bytes_accessed=2_000_000,transcendentals=2_000_000),name="middle")(edges,full,rate)
    return pl.pallas_call(rim_kernel,out_shape=shape(16,16,128),in_specs=[smem]+[vmem]*5,
        scratch_shapes=[pltpu.VMEM((12,2,8,128),F),pltpu.VMEM((5,8,128),F),pltpu.VMEM((4,2,8,128),F)]+scratch(4),compiler_params=params(),name="rim")(
        edges,rim,left,right,rate,mid)
def solution(mesh):
    placed=(P(None,"gx","gy"),P())
    return jax.shard_map(per_device,mesh=mesh,in_specs=placed,out_specs=P(None,"gx","gy"),check_vma=False)
```

```python
import math

import jax
import jax.numpy as jnp
from jax import lax
from jax.experimental import pallas as pl
from jax.experimental.pallas import tpu as pltpu
from jax.sharding import PartitionSpec as P

F = jnp.float32
B = jnp.bfloat16
HALO = 4


def lanes():
    return lax.broadcasted_iota(jnp.int32, (8, 128), 1)


def lane_roll(value, steps):
    steps %= 128
    return pltpu.roll(value, steps, 1) if steps else value


def offsets(shift_z, sy):
    if shift_z:
        return (-2, -1, 0, 1, 2)
    return (0, 1, 2) if sy > 2 else (1, 2)


def moved_row(copies, sy, row, shift_z, parity):
    k = shift_z + parity
    return copies[sy, row, k % 2, k // 2 : k // 2 + 8]


def fill_copies(copies, count, row):
    flat = copies.reshape(5 * count * 2 * 16, 128)
    for slot in range(0, 10 * count, 8):
        flat[pl.ds(16 * slot + 8, 8, stride=16)] = jnp.zeros((8, 128), F)
    for x in range(count):
        for parity in range(2):
            value = row(x, parity)
            for sy in range(5):
                copies[sy, x, parity, 0:8] = lane_roll(value, 2 - sy)


def fill_below(below, squares, blocks):
    count = below.shape[1]
    for sy in range(5):
        for x in range(count):
            for j in range(3):
                below[sy, x, j] = jnp.zeros((8, 128), F)
    flat = below.reshape(5 * count * 3 * 8, 128)
    for source, target, many in blocks:
        sums = []
        for parity in range(2):
            total = squares[parity, source : source + many]
            for step in range(1, 5):
                total = total + squares[parity, source + step : source + step + many]
            near = lane_roll(total, 1) + lane_roll(total, 127)
            far = lane_roll(total, 2) + lane_roll(total, 126)
            sums.append(total + near + far)
        three = (sums[0], sums[0] + sums[1], sums[1])
        for j in range(3):
            for sy in range(5):
                flat[pl.ds(((sy * count + target) * 3 + j) * 8, many, stride=24)] = lane_roll(three[j], 2 - sy)


def put_squares(squares, at, ref, count):
    flat = ref.reshape(count * 16, 128)
    for parity in range(2):
        for start in range(0, count, 8):
            many = min(8, count - start)
            value = flat[pl.ds(parity * 8 + 16 * start, many, stride=16)]
            squares[parity, at + start : at + start + many] = value * value


def clear_sides(sides):
    slots = sides.shape[0] * sides.shape[1] * 3
    flat = sides.reshape(slots * 24, 128)
    for slot in range(0, slots, 8):
        flat[pl.ds(24 * slot + 7, 8, stride=24)] = jnp.zeros((8, 128), F)
        flat[pl.ds(24 * slot + 16, 8, stride=24)] = jnp.zeros((8, 128), F)


def patch_sums(rows, row, moved, sides, parts, base):
    first, count = rows
    squared, pairs, fours = {}, {}, {}

    def square(m):
        if m not in squared:
            x = first - 2 + m
            differences = [row(x, parity) - moved(x, parity) for parity in range(2)]
            squared[m] = [d * d for d in differences]
        return squared[m]

    def pair(m):
        if m not in pairs:
            pairs[m] = [a + b for a, b in zip(square(m), square(m + 1))]
        return pairs[m]

    def four(m):
        if m not in fours:
            fours[m] = [a + b for a, b in zip(pair(m), pair(m + 2))]
        return fours[m]

    for j in range(count):
        shared, other = (four(j + 1), square(j)) if j % 2 == 0 else (four(j), square(j + 4))
        even, odd = [a + b for a, b in zip(shared, other)]
        both = even + odd
        sides[j, 0, 8:16] = both
        sides[j, 1, 8:16] = even
        sides[j, 2, 8:16] = odd
        even = both + sides[j, 0, 7:15] + sides[j, 1, 9:17]
        odd = both + sides[j, 0, 9:17] + sides[j, 2, 7:15]
        sums = jnp.concatenate([even, odd], 0)
        high = sums.astype(B)
        at = base + 16 * j
        parts[at : at + 16, 0:128] = high
        parts[at : at + 16, 128:256] = (sums - high.astype(F)).astype(B)


def accumulate(nx, segments, row, moved, below, rates, masks, column_mask, start, scratch):
    sides, parts, kept, carry, weighted, totals = scratch
    last_slice = lax.broadcasted_iota(jnp.int32, (8, 128), 0) == 7
    clear_sides(sides)
    carry_flat = carry.reshape(2 * nx * 4 * 16, 128)
    for slot in range(0, 8 * nx, 8):
        carry_flat[pl.ds(16 * slot + 7, 8, stride=16)] = jnp.zeros((8, 128), F)
    for x in range(nx):
        for parity in range(2):
            weighted[x, parity], totals[x, parity] = start(x, parity)
    line = lax.broadcasted_iota(jnp.int32, (256, 128), 0) % 128
    column = lax.broadcasted_iota(jnp.int32, (256, 128), 1)
    band = jnp.where(abs(line - column) <= 2, 1.0, 0.0).astype(B)
    for sy in range(5):
        place = {}
        for shift_z in range(3):
            base, todo = 0, []
            for n, shift_x in enumerate(offsets(shift_z, sy)):
                slot = 0
                for rows in segments(shift_x):
                    patch_sums(
                        rows,
                        row,
                        lambda x, parity: moved(sy, x + shift_x, shift_z, parity),
                        sides.at[n, slot : slot + rows[1]],
                        parts,
                        base,
                    )
                    todo.append((shift_x, rows, base, n, slot))
                    base += 16 * rows[1]
                    slot += rows[1]
            sums = jnp.dot(parts[0:base], band, preferred_element_type=F)
            for shift_x, rows, at, n, slot in todo:
                for j in range(rows[1]):
                    x = rows[0] + j
                    for parity in range(2):
                        distance = sums[at + 16 * j + 8 * parity : at + 16 * j + 8 * parity + 8]
                        if shift_z:
                            distance = distance + below(sy, x + shift_x, (shift_z - 1) * (1 + parity))
                        weight = jnp.exp2(distance * rates[parity])
                        if x < 0 or x + shift_x < 0:
                            weight = weight * masks[0]
                        if x >= nx or x + shift_x >= nx:
                            weight = weight * masks[1]
                        if column_mask is not None:
                            weight = weight * column_mask[sy]
                        spot = (sy % 2, shift_z * 5 + n, slot + j, parity)
                        kept[spot] = weight
                        place[shift_z, shift_x, x, parity] = spot
        for x in range(nx):
            gather(sy, x, place, row, moved, kept, carry.at[sy % 2, x], last_slice, weighted, totals)


def plus(a, b):
    return b if a is None else a if b is None else a + b


def gather(sy, x, place, row, moved, kept, carry, last_slice, weighted, totals):
    ahead = [[None, None], [None, None]]
    back = [[[None, None] for _ in range(3)] for _ in range(2)]
    for shift_z in range(3):
        count = [None, None]
        for shift_x in offsets(shift_z, sy):
            for parity in range(2):
                spot = place.get((shift_z, shift_x, x, parity))
                if spot is not None:
                    weight = kept[spot]
                    ahead[0][parity] = plus(ahead[0][parity], weight * moved(sy, x + shift_x, shift_z, parity))
                    count[parity] = plus(count[parity], weight)
                spot = place.get((shift_z, shift_x, x - shift_x, parity))
                if spot is not None:
                    weight = kept[spot]
                    back[0][shift_z][parity] = plus(back[0][shift_z][parity], weight * row(x - shift_x, parity))
                    back[1][shift_z][parity] = plus(back[1][shift_z][parity], weight)
        for parity in range(2):
            if shift_z + parity >= 2 and count[parity] is not None:
                count[parity] = jnp.where(last_slice, 0.0, count[parity])
            ahead[1][parity] = plus(ahead[1][parity], count[parity])
    for m, total in enumerate((weighted, totals)):
        here = [plus(back[m][0][0], None), plus(back[m][0][1], back[m][1][0])]
        for parity, up in enumerate((plus(back[m][1][1], back[m][2][0]), back[m][2][1])):
            if up is not None:
                carry[2 * m + parity, 8:16] = up
                here[parity] = plus(here[parity], carry[2 * m + parity, 7:15])
        for parity in range(2):
            term = ahead[m][parity]
            if here[parity] is not None:
                term = plus(term, lane_roll(here[parity], sy - 2))
            if term is not None:
                total[x, parity] = total[x, parity] + term


def work(nx, rows):
    return [
        pltpu.VMEM((5, rows, 3, 24, 128), F),
        pltpu.VMEM((5 * 16 * rows, 256), B),
        pltpu.VMEM((2, 15, rows, 2, 8, 128), F),
        pltpu.VMEM((2, nx, 4, 16, 128), F),
    ]


def pack_kernel(strength_ref, noisy_ref, own_ref, first_ref, last_ref, rate_ref):
    flat = noisy_ref.reshape(256, 128)
    for x in range(16):
        for parity in range(2):
            value = flat[pl.ds(parity * 16 + x, 8, stride=32)]
            own_ref[x, parity] = value
            if x < HALO:
                first_ref[x, parity] = value
            if x >= 16 - HALO:
                last_ref[x - 16 + HALO, parity] = value
    sublane = lax.broadcasted_iota(jnp.int32, (8, 128), 0)
    for parity in range(2):
        strength = jnp.full((8, 128), 1.0, F)
        for s in range(8):
            strength = jnp.where(sublane == s, strength_ref[2 * s + parity], strength)
        rate_ref[parity] = (-math.log2(math.e) / 125.0) / strength


def inner_segments(shift_x):
    return ((2 + max(0, -shift_x), 12 - abs(shift_x)),)


def outer_segments(shift_x):
    many = 2 + abs(shift_x)
    return ((-max(0, shift_x), many), (14 - max(0, shift_x), many))


def whole_segments(nx):
    return lambda shift_x: ((-max(0, shift_x), nx + abs(shift_x)),)


def to_strips(value, chunk):
    lane = lanes() - 32 * chunk
    right = jnp.where((lane >= 16) & (lane < 24), lane_roll(value, 24 + 32 * chunk), 0.0)
    return jnp.where((lane >= 4) & (lane < 12), lane_roll(value, 4 + 32 * chunk), right)


def inner_kernel(own_ref, rate_ref, copies, weighted, totals, rim_ref, left_ref, right_ref, below, squares, *scratch):
    def row(x, parity):
        return own_ref[x, parity]

    fill_copies(copies, 16, row)
    put_squares(squares, 0, own_ref, 16)
    fill_below(below, squares, ((0, 0, 8), (8, 8, 4)))
    lane = lanes()
    place = (lane % 32) // 4
    for x in range(12):
        for parity in range(2):
            value = jnp.zeros((8, 128), F)
            for chunk in range(4):
                source = 4 * chunk + x - HALO
                if 0 <= source < 16:
                    value = value + to_strips(own_ref[source, parity], chunk)
            rim_ref[x, parity] = value
    for group in range(3):
        for ref, column in ((left_ref, 0), (right_ref, 124)):
            message = jnp.zeros((8, 128), F)
            for chunk in range(4):
                for slot in range(8):
                    source = 4 * chunk + 4 * group + slot // 2 - HALO
                    if 0 <= source < 16:
                        here = (place == slot) & (lane // 32 == chunk)
                        message = jnp.where(here, lane_roll(own_ref[source, slot % 2], 32 * chunk + 4 * slot - column), message)
            ref[group] = message
    one = jnp.ones((8, 128), F)
    accumulate(
        16,
        inner_segments,
        row,
        lambda sy, x, shift_z, parity: moved_row(copies, sy, x, shift_z, parity),
        lambda sy, x, j: below[sy, x - 2, j],
        (rate_ref[0], rate_ref[1]),
        None,
        None,
        lambda x, parity: (own_ref[x, parity], one),
        (*scratch, weighted, totals),
    )


def join_kernel(low_ref, high_ref, rim_ref, left_ref, right_ref, rim_out, left_out, right_out):
    lane = lanes()
    place = (lane % 32) // 4
    for x in range(12):
        for parity in range(2):
            value = rim_ref[x, parity]
            if x < HALO:
                value = value + to_strips(low_ref[x, parity], 0)
            if x >= 8:
                value = value + to_strips(high_ref[x - 8, parity], 3)
            rim_out[x, parity] = value
    for ref, out, column in ((left_ref, left_out, 0), (right_ref, right_out, 124)):
        out[1] = ref[1]
        for group, halo, chunk in ((0, low_ref, 0), (2, high_ref, 3)):
            message = ref[group]
            for slot in range(8):
                here = (place == slot) & (lane // 32 == chunk)
                message = jnp.where(here, lane_roll(halo[slot // 2, slot % 2], 32 * chunk + 4 * slot - column), message)
            out[group] = message


def outer_kernel(edge_ref, own_ref, low_ref, high_ref, copies, rate_ref, inner_w, inner_t, mid_ref, far, below, squares, halo, *scratch):
    def row(x, parity):
        if x < 0:
            return low_ref[x + HALO, parity]
        return own_ref[x, parity] if x < 16 else high_ref[x - 16, parity]

    def moved(sy, x, shift_z, parity):
        if 0 <= x < 16:
            return moved_row(copies, sy, x, shift_z, parity)
        return moved_row(far, sy, x + HALO if x < 0 else x - 12, shift_z, parity)

    def taken(sy, x, j):
        return below[sy, x + 2 if x < 6 else x - 2, j]

    fill_copies(far, 8, lambda x, parity: row(x - HALO if x < HALO else x + 12, parity))
    put_squares(squares, 0, low_ref, 4)
    put_squares(squares, 4, own_ref, 16)
    put_squares(squares, 20, high_ref, 4)
    fill_below(below, squares, ((0, 0, 8), (12, 8, 8)))
    one = jnp.ones((8, 128), F)
    accumulate(
        16,
        outer_segments,
        row,
        moved,
        taken,
        (rate_ref[0], rate_ref[1]),
        (one * edge_ref[0], one * edge_ref[1]),
        None,
        lambda x, parity: (inner_w[x, parity], inner_t[x, parity]),
        scratch,
    )
    for x in range(16):
        for parity in range(2):
            mid_ref[x, parity] = scratch[-2][x, parity] / scratch[-1][x, parity]


def rim_kernel(edge_ref, rim_ref, left_ref, right_ref, rate_ref, mid_ref, out_ref, rows, copies, below, squares, column_mask, *scratch):
    lane = lanes()
    spot = lane % 32
    for x in range(12):
        group, slot = x // 4, (x % 4) * 2
        for parity in range(2):
            value = rim_ref[x, parity]
            value = jnp.where(spot < 4, lane_roll(left_ref[group], -4 * (slot + parity)), value)
            rows[x, parity] = jnp.where((spot >= 24) & (spot < 28), lane_roll(right_ref[group], 24 - 4 * (slot + parity)), value)
    for sy in range(5):
        off_left = (spot < 4) | ((spot + sy - 2 < 4) & (spot < 16))
        c = spot - 16
        off_right = (c >= 8) | ((c + sy - 2 >= 8) & (c >= 0))
        column_mask[sy] = jnp.where(off_left, edge_ref[2], 1.0) * jnp.where(off_right, edge_ref[3], 1.0)

    def row(x, parity):
        return rows[x + HALO, parity]

    fill_copies(copies, 12, lambda x, parity: rows[x, parity])
    put_squares(squares, 0, rows, 12)
    fill_below(below, squares, ((0, 0, 8),))
    one = jnp.ones((8, 128), F)
    accumulate(
        4,
        whole_segments(4),
        row,
        lambda sy, x, shift_z, parity: moved_row(copies, sy, x + HALO, shift_z, parity),
        lambda sy, x, j: below[sy, x + 2, j],
        (rate_ref[0], rate_ref[1]),
        (jnp.where(lane < 32, edge_ref[0], 1.0), jnp.where(lane >= 96, edge_ref[1], 1.0)),
        column_mask,
        lambda x, parity: (rows[x + HALO, parity], one),
        scratch,
    )
    flat = out_ref.reshape(256, 128)
    for x in range(4):
        for parity in range(2):
            value = scratch[-2][x, parity] / scratch[-1][x, parity]
            for chunk in range(4):
                at = 4 * chunk + x
                edge = jnp.where(lane < 4, lane_roll(value, -32 * chunk - 4), lane_roll(value, 104 - 32 * chunk))
                flat[pl.ds(parity * 16 + at, 8, stride=32)] = jnp.where((lane < 4) | (lane >= 124), edge, mid_ref[at, parity])


def shape(*dims):
    return jax.ShapeDtypeStruct(dims, F)


def call(kernel, name, outs, scratch, mib, in_specs, flops=0):
    return pl.pallas_call(
        kernel,
        out_shape=outs,
        in_specs=[pl.BlockSpec(memory_space=pltpu.SMEM if s else pltpu.VMEM) for s in in_specs],
        out_specs=jax.tree.map(lambda _: pl.BlockSpec(memory_space=pltpu.VMEM), outs),
        scratch_shapes=scratch,
        compiler_params=pltpu.CompilerParams(vmem_limit_bytes=mib * 2**20),
        cost_estimate=pl.CostEstimate(flops=flops, bytes_accessed=500_000, transcendentals=0),
        name=name,
    )


def passed_along(value, axis, steps):
    count = lax.axis_size(axis)
    first, last = max(0, -steps), min(count, count - steps)
    return lax.ppermute(value, axis, [(a, a + steps) for a in range(first, last)])


def per_device(noisy, strength):
    V = pltpu.VMEM
    gx, gy = lax.axis_index("gx"), lax.axis_index("gy")
    edges = jnp.stack([gx > 0, gx < lax.axis_size("gx") - 1, gy > 0, gy < lax.axis_size("gy") - 1]).astype(F)
    row4, row12, row16, three = shape(4, 2, 8, 128), shape(12, 2, 8, 128), shape(16, 2, 8, 128), shape(3, 8, 128)
    copied = (5, 16, 2, 16, 128)
    own, first, last, rate = call(pack_kernel, "pack", (row16, row4, row4, shape(2, 8, 128)), [], 4, (1, 0))(strength, noisy)
    low = passed_along(last, "gx", 1)
    high = passed_along(first, "gx", -1)
    copies, inner_w, inner_t, rim, to_left, to_right = call(
        inner_kernel,
        "inner",
        (shape(*copied), row16, row16, row12, three, three),
        [V((5, 12, 3, 8, 128), F), V((2, 24, 128), F)] + work(16, 16),
        20,
        (0, 0),
        60_000_000,
    )(own, rate)
    rim, to_left, to_right = call(join_kernel, "join", (row12, three, three), [], 4, (0,) * 5)(low, high, rim, to_left, to_right)
    left = passed_along(to_right, "gy", 1)
    right = passed_along(to_left, "gy", -1)
    mid = call(
        outer_kernel,
        "outer",
        row16,
        [V((5, 8, 2, 16, 128), F), V((5, 16, 3, 8, 128), F), V((2, 32, 128), F), V((8, 128), F)]
        + work(16, 8)
        + [V((16, 2, 8, 128), F)] * 2,
        20,
        (1,) + (0,) * 7,
        40_000_000,
    )(edges, own, low, high, copies, rate, inner_w, inner_t)
    return call(
        rim_kernel,
        "rim",
        shape(16, 16, 128),
        [V((12, 2, 8, 128), F), V((5, 12, 2, 16, 128), F), V((5, 8, 3, 8, 128), F), V((2, 24, 128), F), V((5, 8, 128), F)]
        + work(4, 8)
        + [V((4, 2, 8, 128), F)] * 2,
        20,
        (1,) + (0,) * 5,
        20_000_000,
    )(edges, rim, left, right, rate, mid)


def solution(mesh):
    placed = (P(None, "gx", "gy"), P())
    return jax.shard_map(per_device, mesh=mesh, in_specs=placed, out_specs=P(None, "gx", "gy"), check_vma=False)
```

```python
import math

import jax
import jax.numpy as jnp
from jax import lax
from jax.experimental import pallas as pl
from jax.experimental.pallas import tpu as pltpu
from jax.sharding import PartitionSpec as P

F = jnp.float32
B = jnp.bfloat16
HALO = 4


def lanes():
    return lax.broadcasted_iota(jnp.int32, (8, 128), 1)


def lane_roll(value, steps):
    steps %= 128
    return pltpu.roll(value, steps, 1) if steps else value


def offsets(shift_z, sy):
    if shift_z:
        return (-2, -1, 0, 1, 2)
    return (0, 1, 2) if sy > 2 else (1, 2)


def moved_row(copies, sy, row, shift_z, parity):
    k = shift_z + parity
    return copies[sy, row, k % 2, k // 2 : k // 2 + 8]


def fill_copies(copies, count, row):
    flat = copies.reshape(5 * count * 2 * 16, 128)
    for slot in range(0, 10 * count, 8):
        flat[pl.ds(16 * slot + 8, 8, stride=16)] = jnp.zeros((8, 128), F)
    for x in range(count):
        for parity in range(2):
            value = row(x, parity)
            for sy in range(5):
                copies[sy, x, parity, 0:8] = lane_roll(value, 2 - sy)


def fill_below(below, squares, blocks):
    count = below.shape[1]
    for sy in range(5):
        for x in range(count):
            for j in range(3):
                below[sy, x, j] = jnp.zeros((8, 128), F)
    flat = below.reshape(5 * count * 3 * 8, 128)
    for source, target, many in blocks:
        sums = []
        for parity in range(2):
            total = squares[parity, source : source + many]
            for step in range(1, 5):
                total = total + squares[parity, source + step : source + step + many]
            near = lane_roll(total, 1) + lane_roll(total, 127)
            far = lane_roll(total, 2) + lane_roll(total, 126)
            sums.append(total + near + far)
        three = (sums[0], sums[0] + sums[1], sums[1])
        for j in range(3):
            for sy in range(5):
                flat[pl.ds(((sy * count + target) * 3 + j) * 8, many, stride=24)] = lane_roll(three[j], 2 - sy)


def put_squares(squares, at, ref, count):
    flat = ref.reshape(count * 16, 128)
    for parity in range(2):
        for start in range(0, count, 8):
            many = min(8, count - start)
            value = flat[pl.ds(parity * 8 + 16 * start, many, stride=16)]
            squares[parity, at + start : at + start + many] = value * value


def clear_sides(sides):
    slots = sides.shape[0] * sides.shape[1] * 3
    flat = sides.reshape(slots * 24, 128)
    for slot in range(0, slots, 8):
        flat[pl.ds(24 * slot + 7, 8, stride=24)] = jnp.zeros((8, 128), F)
        flat[pl.ds(24 * slot + 16, 8, stride=24)] = jnp.zeros((8, 128), F)


def patch_sums(rows, row, moved, sides, parts, base):
    first, count = rows
    squared, pairs, fours = {}, {}, {}

    def square(m):
        if m not in squared:
            x = first - 2 + m
            differences = [row(x, parity) - moved(x, parity) for parity in range(2)]
            squared[m] = [d * d for d in differences]
        return squared[m]

    def pair(m):
        if m not in pairs:
            pairs[m] = [a + b for a, b in zip(square(m), square(m + 1))]
        return pairs[m]

    def four(m):
        if m not in fours:
            fours[m] = [a + b for a, b in zip(pair(m), pair(m + 2))]
        return fours[m]

    for j in range(count):
        shared, other = (four(j + 1), square(j)) if j % 2 == 0 else (four(j), square(j + 4))
        even, odd = [a + b for a, b in zip(shared, other)]
        both = even + odd
        sides[j, 0, 8:16] = both
        sides[j, 1, 8:16] = even
        sides[j, 2, 8:16] = odd
        even = both + sides[j, 0, 7:15] + sides[j, 1, 9:17]
        odd = both + sides[j, 0, 9:17] + sides[j, 2, 7:15]
        sums = jnp.concatenate([even, odd], 0)
        high = sums.astype(B)
        at = base + 16 * j
        parts[at : at + 16, 0:128] = high
        parts[at : at + 16, 128:256] = (sums - high.astype(F)).astype(B)


def accumulate(nx, segments, row, moved, below, rates, masks, column_mask, start, scratch):
    sides, parts, kept, carry, weighted, totals = scratch
    last_slice = lax.broadcasted_iota(jnp.int32, (8, 128), 0) == 7
    clear_sides(sides)
    carry_flat = carry.reshape(2 * nx * 4 * 16, 128)
    for slot in range(0, 8 * nx, 8):
        carry_flat[pl.ds(16 * slot + 7, 8, stride=16)] = jnp.zeros((8, 128), F)
    for x in range(nx):
        for parity in range(2):
            weighted[x, parity], totals[x, parity] = start(x, parity)
    line = lax.broadcasted_iota(jnp.int32, (256, 128), 0) % 128
    column = lax.broadcasted_iota(jnp.int32, (256, 128), 1)
    band = jnp.where(abs(line - column) <= 2, 1.0, 0.0).astype(B)
    for sy in range(5):
        place = {}
        for shift_z in range(3):
            base, todo = 0, []
            for n, shift_x in enumerate(offsets(shift_z, sy)):
                slot = 0
                for rows in segments(shift_x):
                    patch_sums(
                        rows,
                        row,
                        lambda x, parity: moved(sy, x + shift_x, shift_z, parity),
                        sides.at[n, slot : slot + rows[1]],
                        parts,
                        base,
                    )
                    todo.append((shift_x, rows, base, n, slot))
                    base += 16 * rows[1]
                    slot += rows[1]
            sums = jnp.dot(parts[0:base], band, preferred_element_type=F)
            for shift_x, rows, at, n, slot in todo:
                for j in range(rows[1]):
                    x = rows[0] + j
                    for parity in range(2):
                        distance = sums[at + 16 * j + 8 * parity : at + 16 * j + 8 * parity + 8]
                        if shift_z:
                            distance = distance + below(sy, x + shift_x, (shift_z - 1) * (1 + parity))
                        weight = jnp.exp2(distance * rates[parity])
                        if x < 0 or x + shift_x < 0:
                            weight = weight * masks[0]
                        if x >= nx or x + shift_x >= nx:
                            weight = weight * masks[1]
                        if column_mask is not None:
                            weight = weight * column_mask[sy]
                        spot = (sy % 2, shift_z * 5 + n, slot + j, parity)
                        kept[spot] = weight
                        place[shift_z, shift_x, x, parity] = spot
        for x in range(nx):
            gather(sy, x, place, row, moved, kept, carry.at[sy % 2, x], last_slice, weighted, totals)


def plus(a, b):
    return b if a is None else a if b is None else a + b


def gather(sy, x, place, row, moved, kept, carry, last_slice, weighted, totals):
    ahead = [[None, None], [None, None]]
    back = [[[None, None] for _ in range(3)] for _ in range(2)]
    for shift_z in range(3):
        count = [None, None]
        for shift_x in offsets(shift_z, sy):
            for parity in range(2):
                spot = place.get((shift_z, shift_x, x, parity))
                if spot is not None:
                    weight = kept[spot]
                    ahead[0][parity] = plus(ahead[0][parity], weight * moved(sy, x + shift_x, shift_z, parity))
                    count[parity] = plus(count[parity], weight)
                spot = place.get((shift_z, shift_x, x - shift_x, parity))
                if spot is not None:
                    weight = kept[spot]
                    back[0][shift_z][parity] = plus(back[0][shift_z][parity], weight * row(x - shift_x, parity))
                    back[1][shift_z][parity] = plus(back[1][shift_z][parity], weight)
        for parity in range(2):
            if shift_z + parity >= 2 and count[parity] is not None:
                count[parity] = jnp.where(last_slice, 0.0, count[parity])
            ahead[1][parity] = plus(ahead[1][parity], count[parity])
    for m, total in enumerate((weighted, totals)):
        here = [plus(back[m][0][0], None), plus(back[m][0][1], back[m][1][0])]
        for parity, up in enumerate((plus(back[m][1][1], back[m][2][0]), back[m][2][1])):
            if up is not None:
                carry[2 * m + parity, 8:16] = up
                here[parity] = plus(here[parity], carry[2 * m + parity, 7:15])
        for parity in range(2):
            term = ahead[m][parity]
            if here[parity] is not None:
                term = plus(term, lane_roll(here[parity], sy - 2))
            if term is not None:
                total[x, parity] = total[x, parity] + term


def work(nx, rows):
    return [
        pltpu.VMEM((5, rows, 3, 24, 128), F),
        pltpu.VMEM((5 * 16 * rows, 256), B),
        pltpu.VMEM((2, 15, rows, 2, 8, 128), F),
        pltpu.VMEM((2, nx, 4, 16, 128), F),
    ]


def inner_segments(shift_x):
    return ((2 + max(0, -shift_x), 12 - abs(shift_x)),)


def outer_segments(shift_x):
    many = 2 + abs(shift_x)
    return ((-max(0, shift_x), many), (14 - max(0, shift_x), many))


def whole_segments(nx):
    return lambda shift_x: ((-max(0, shift_x), nx + abs(shift_x)),)


def to_strips(value, chunk):
    lane = lanes() - 32 * chunk
    right = jnp.where((lane >= 16) & (lane < 24), lane_roll(value, 24 + 32 * chunk), 0.0)
    return jnp.where((lane >= 4) & (lane < 12), lane_roll(value, 4 + 32 * chunk), right)


def inner_kernel(noisy_ref, strength_ref, own_ref, rate_ref, copies, weighted, totals, rim_ref, left_ref, right_ref, below, squares, *scratch):
    def row(x, parity):
        return own_ref[x, parity]

    flat = noisy_ref.reshape(256, 128)
    for x in range(16):
        for parity in range(2):
            own_ref[x, parity] = flat[pl.ds(parity * 16 + x, 8, stride=32)]
    slices = jnp.broadcast_to(strength_ref[...], (8, 16))
    sublane, lane = [lax.broadcasted_iota(jnp.int32, (8, 16), dim) for dim in range(2)]
    for parity in range(2):
        strength = jnp.sum(jnp.where(lane == 2 * sublane + parity, slices, 0.0), axis=1, keepdims=True)
        rate_ref[parity] = jnp.broadcast_to((-math.log2(math.e) / 125.0) / strength, (8, 128))

    fill_copies(copies, 16, row)
    put_squares(squares, 0, own_ref, 16)
    fill_below(below, squares, ((0, 0, 8), (8, 8, 4)))
    lane = lanes()
    place = (lane % 32) // 4
    for x in range(12):
        for parity in range(2):
            value = jnp.zeros((8, 128), F)
            for chunk in range(4):
                source = 4 * chunk + x - HALO
                if 0 <= source < 16:
                    value = value + to_strips(own_ref[source, parity], chunk)
            rim_ref[x, parity] = value
    for group in range(3):
        for ref, column in ((left_ref, 0), (right_ref, 124)):
            message = jnp.zeros((8, 128), F)
            for chunk in range(4):
                for slot in range(8):
                    source = 4 * chunk + 4 * group + slot // 2 - HALO
                    if 0 <= source < 16:
                        here = (place == slot) & (lane // 32 == chunk)
                        message = jnp.where(here, lane_roll(own_ref[source, slot % 2], 32 * chunk + 4 * slot - column), message)
            ref[group] = message
    one = jnp.ones((8, 128), F)
    accumulate(
        16,
        inner_segments,
        row,
        lambda sy, x, shift_z, parity: moved_row(copies, sy, x, shift_z, parity),
        lambda sy, x, j: below[sy, x - 2, j],
        (rate_ref[0], rate_ref[1]),
        None,
        None,
        lambda x, parity: (own_ref[x, parity], one),
        (*scratch, weighted, totals),
    )


def join_kernel(flag_ref, pair_ref, next_ref, rim_ref, left_ref, right_ref, low_ref, high_ref, rim_out, first_out, second_out):
    odd = flag_ref[4] > 0.5
    pair, other = pair_ref.reshape(256, 128), next_ref.reshape(256, 128)
    for x in range(HALO):
        for parity in range(2):
            line = pl.ds(parity * 16 + 12 + x, 8, stride=32)
            low_ref[x, parity] = jnp.where(odd, pair[line], other[line])
            line = pl.ds(parity * 16 + x, 8, stride=32)
            high_ref[x, parity] = jnp.where(odd, other[line], pair[line])
    lane = lanes()
    place = (lane % 32) // 4
    for x in range(12):
        for parity in range(2):
            value = rim_ref[x, parity]
            if x < HALO:
                value = value + to_strips(low_ref[x, parity], 0)
            if x >= 8:
                value = value + to_strips(high_ref[x - 8, parity], 3)
            rim_out[x, parity] = value
    messages = []
    for ref, column in ((left_ref, 0), (right_ref, 124)):
        groups = [ref[0], ref[1], ref[2]]
        for group, halo, chunk in ((0, low_ref, 0), (2, high_ref, 3)):
            for slot in range(8):
                here = (place == slot) & (lane // 32 == chunk)
                piece = lane_roll(halo[slot // 2, slot % 2], 32 * chunk + 4 * slot - column)
                groups[group] = jnp.where(here, piece, groups[group])
        messages.append(groups)
    odd = flag_ref[5] > 0.5
    for group in range(3):
        left, right = messages[0][group], messages[1][group]
        first_out[group] = jnp.where(odd, left, right)
        second_out[group] = jnp.where(odd, right, left)


def outer_kernel(flag_ref, own_ref, low_ref, high_ref, copies, rate_ref, inner_w, inner_t, mid_ref, far, below, squares, halo, *scratch):
    def row(x, parity):
        if x < 0:
            return low_ref[x + HALO, parity]
        return own_ref[x, parity] if x < 16 else high_ref[x - 16, parity]

    def moved(sy, x, shift_z, parity):
        if 0 <= x < 16:
            return moved_row(copies, sy, x, shift_z, parity)
        return moved_row(far, sy, x + HALO if x < 0 else x - 12, shift_z, parity)

    def taken(sy, x, j):
        return below[sy, x + 2 if x < 6 else x - 2, j]

    fill_copies(far, 8, lambda x, parity: row(x - HALO if x < HALO else x + 12, parity))
    put_squares(squares, 0, low_ref, 4)
    put_squares(squares, 4, own_ref, 16)
    put_squares(squares, 20, high_ref, 4)
    fill_below(below, squares, ((0, 0, 8), (12, 8, 8)))
    one = jnp.ones((8, 128), F)
    accumulate(
        16,
        outer_segments,
        row,
        moved,
        taken,
        (rate_ref[0], rate_ref[1]),
        (flag_ref[0], flag_ref[1]),
        None,
        lambda x, parity: (inner_w[x, parity], inner_t[x, parity]),
        scratch,
    )
    for x in range(16):
        for parity in range(2):
            mid_ref[x, parity] = scratch[-2][x, parity] / scratch[-1][x, parity]


def rim_kernel(flag_ref, rim_ref, first_ref, second_ref, rate_ref, mid_ref, out_ref, rows, copies, below, squares, column_mask, *scratch):
    lane = lanes()
    spot = lane % 32
    odd = flag_ref[5] > 0.5
    sides = [(first_ref[group], second_ref[group]) for group in range(3)]
    lefts = [jnp.where(odd, a, b) for a, b in sides]
    rights = [jnp.where(odd, b, a) for a, b in sides]
    for x in range(12):
        group, slot = x // 4, (x % 4) * 2
        for parity in range(2):
            value = rim_ref[x, parity]
            value = jnp.where(spot < 4, lane_roll(lefts[group], -4 * (slot + parity)), value)
            rows[x, parity] = jnp.where((spot >= 24) & (spot < 28), lane_roll(rights[group], 24 - 4 * (slot + parity)), value)
    for sy in range(5):
        off_left = (spot < 4) | ((spot + sy - 2 < 4) & (spot < 16))
        c = spot - 16
        off_right = (c >= 8) | ((c + sy - 2 >= 8) & (c >= 0))
        column_mask[sy] = jnp.where(off_left, flag_ref[2], 1.0) * jnp.where(off_right, flag_ref[3], 1.0)

    def row(x, parity):
        return rows[x + HALO, parity]

    fill_copies(copies, 12, lambda x, parity: rows[x, parity])
    put_squares(squares, 0, rows, 12)
    fill_below(below, squares, ((0, 0, 8),))
    one = jnp.ones((8, 128), F)
    accumulate(
        4,
        whole_segments(4),
        row,
        lambda sy, x, shift_z, parity: moved_row(copies, sy, x + HALO, shift_z, parity),
        lambda sy, x, j: below[sy, x + 2, j],
        (rate_ref[0], rate_ref[1]),
        (jnp.where(lane < 32, flag_ref[0], 1.0), jnp.where(lane >= 96, flag_ref[1], 1.0)),
        column_mask,
        lambda x, parity: (rows[x + HALO, parity], one),
        scratch,
    )
    flat = out_ref.reshape(256, 128)
    for x in range(4):
        for parity in range(2):
            value = scratch[-2][x, parity] / scratch[-1][x, parity]
            for chunk in range(4):
                at = 4 * chunk + x
                edge = jnp.where(lane < 4, lane_roll(value, -32 * chunk - 4), lane_roll(value, 104 - 32 * chunk))
                flat[pl.ds(parity * 16 + at, 8, stride=32)] = jnp.where((lane < 4) | (lane >= 124), edge, mid_ref[at, parity])


def shape(*dims):
    return jax.ShapeDtypeStruct(dims, F)


def call(kernel, name, outs, scratch, mib, flops=0):
    spec = pl.BlockSpec(memory_space=pltpu.VMEM)
    return pl.pallas_call(
        kernel,
        out_shape=outs,
        out_specs=jax.tree.map(lambda _: spec, outs),
        in_specs=INPUTS[name] * [spec],
        scratch_shapes=scratch,
        compiler_params=pltpu.CompilerParams(vmem_limit_bytes=mib * 2**20),
        cost_estimate=pl.CostEstimate(flops=flops, bytes_accessed=500_000, transcendentals=0),
        name=name,
    )


INPUTS = {"inner": 2, "join": 6, "outer": 8, "rim": 6}


def swapped(value, axis, first):
    pairs = [(a, a + 1) for a in range(first, lax.axis_size(axis) - 1, 2)]
    return lax.ppermute(value, axis, pairs + [(b, a) for a, b in pairs])


def per_device(noisy, strength):
    V = pltpu.VMEM
    gx, gy = lax.axis_index("gx"), lax.axis_index("gy")
    flags = [gx > 0, gx < lax.axis_size("gx") - 1, gy > 0, gy < lax.axis_size("gy") - 1, gx % 2 == 1, gy % 2 == 1]
    flags = jnp.broadcast_to(jnp.stack(flags).astype(F)[:, None, None], (6, 8, 128))
    row4, row12, row16, three = shape(4, 2, 8, 128), shape(12, 2, 8, 128), shape(16, 2, 8, 128), shape(3, 8, 128)
    pair = swapped(noisy, "gx", 0)
    other = swapped(noisy, "gx", 1)
    own, rate, copies, inner_w, inner_t, rim, to_left, to_right = call(
        inner_kernel,
        "inner",
        (row16, shape(2, 8, 128), shape(5, 16, 2, 16, 128), row16, row16, row12, three, three),
        [V((5, 12, 3, 8, 128), F), V((2, 24, 128), F)] + work(16, 16),
        20,
        60_000_000,
    )(noisy, strength.reshape(1, 16))
    low, high, rim, first, second = call(join_kernel, "join", (row4, row4, row12, three, three), [], 4)(
        flags, pair, other, rim, to_left, to_right
    )
    first = swapped(first, "gy", 0)
    second = swapped(second, "gy", 1)
    mid = call(
        outer_kernel,
        "outer",
        row16,
        [V((5, 8, 2, 16, 128), F), V((5, 16, 3, 8, 128), F), V((2, 32, 128), F), V((8, 128), F)]
        + work(16, 8)
        + [V((16, 2, 8, 128), F)] * 2,
        20,
        40_000_000,
    )(flags, own, low, high, copies, rate, inner_w, inner_t)
    return call(
        rim_kernel,
        "rim",
        shape(16, 16, 128),
        [V((12, 2, 8, 128), F), V((5, 12, 2, 16, 128), F), V((5, 8, 3, 8, 128), F), V((2, 24, 128), F), V((5, 8, 128), F)]
        + work(4, 8)
        + [V((4, 2, 8, 128), F)] * 2,
        20,
        20_000_000,
    )(flags, rim, first, second, rate, mid)


def solution(mesh):
    placed = (P(None, "gx", "gy"), P())
    return jax.shard_map(per_device, mesh=mesh, in_specs=placed, out_specs=P(None, "gx", "gy"), check_vma=False)
```

```python
import math

import jax
import jax.numpy as jnp
from jax import lax
from jax.experimental import pallas as pl
from jax.experimental.pallas import tpu as pltpu
from jax.sharding import PartitionSpec as P

F = jnp.float32
B = jnp.bfloat16
HALO = 4


def lanes():
    return lax.broadcasted_iota(jnp.int32, (8, 128), 1)


def lane_roll(value, steps):
    steps %= 128
    return pltpu.roll(value, steps, 1) if steps else value


def offsets(shift_z, sy):
    if shift_z:
        return (-2, -1, 0, 1, 2)
    return (0, 1, 2) if sy > 2 else (1, 2)


def moved_row(copies, sy, row, shift_z, parity):
    return copies[sy, row, shift_z + parity]


def fill_copies(copies, steps, count, row):
    flat = steps.reshape(2 * count * 16, 128)
    for slot in range(0, 2 * count, 8):
        flat[pl.ds(16 * slot + 8, 8, stride=16)] = jnp.zeros((8, 128), F)
    for x in range(count):
        for parity in range(2):
            value = row(x, parity)
            steps[x, parity, 0:8] = value
            up = steps[x, parity, 1:9]
            for sy in range(5):
                copies[sy, x, parity] = lane_roll(value, 2 - sy)
                copies[sy, x, parity + 2] = lane_roll(up, 2 - sy)


def fill_below(below, centers, row):
    squares = {}

    def square(x):
        if x not in squares:
            squares[x] = [row(x, parity) * row(x, parity) for parity in range(2)]
        return squares[x]

    for place, x in enumerate(centers):
        sums = []
        for parity in range(2):
            near = square(x - 1)[parity] + square(x + 1)[parity]
            far = square(x - 2)[parity] + square(x + 2)[parity]
            sums.append(square(x)[parity] + near + far)
        three = (sums[0], sums[0] + sums[1], sums[1])
        for j in range(3):
            for sy in range(5):
                below[sy, place, j] = lane_roll(three[j], 2 - sy)


def patch_sums(rows, row, moved, under, parts):
    first, count = rows
    sub = lax.broadcasted_iota(jnp.int32, (8, 128), 0)
    top, bottom = sub == 0, sub == 7
    squared, pairs, fours = {}, {}, {}

    def square(m):
        if m not in squared:
            x = first - 2 + m
            differences = [row(x, parity) - moved(x, parity) for parity in range(2)]
            squared[m] = [d * d for d in differences]
        return squared[m]

    def pair(m):
        if m not in pairs:
            pairs[m] = [a + b for a, b in zip(square(m), square(m + 1))]
        return pairs[m]

    def four(m):
        if m not in fours:
            fours[m] = [a + b for a, b in zip(pair(m), pair(m + 2))]
        return fours[m]

    for j in range(count):
        shared, other = (four(j + 1), square(j)) if j % 2 == 0 else (four(j), square(j + 4))
        even, odd = [a + b for a, b in zip(shared, other)]
        both = even + odd
        up = jnp.where(top, under(first + j, 0), pltpu.roll(both, 1, 0))
        down = jnp.where(bottom, 0.0, pltpu.roll(both, 7, 0))
        even, odd = (
            both + up + jnp.where(bottom, 0.0, pltpu.roll(even, 7, 0)),
            both + down + jnp.where(top, under(first + j, 1), pltpu.roll(odd, 1, 0)),
        )
        sums = jnp.concatenate([even, odd], 0)
        high = sums.astype(B)
        parts.append(jnp.concatenate([high, (sums - high.astype(F)).astype(B)], 1))


def accumulate(nx, segments, row, moved, below, rates, masks, column_mask, start, scratch):
    kept, carry, weighted, totals = scratch
    last_slice = lax.broadcasted_iota(jnp.int32, (8, 128), 0) == 7
    carry_flat = carry.reshape(2 * nx * 4 * 16, 128)
    for slot in range(0, 8 * nx, 8):
        carry_flat[pl.ds(16 * slot + 7, 8, stride=16)] = jnp.zeros((8, 128), F)
    for x in range(nx):
        for parity in range(2):
            weighted[x, parity], totals[x, parity] = start(x, parity)
    line = lax.broadcasted_iota(jnp.int32, (256, 128), 0) % 128
    column = lax.broadcasted_iota(jnp.int32, (256, 128), 1)
    band = jnp.where(abs(line - column) <= 2, 1.0, 0.0).astype(B)
    for sy in range(5):
        place = {}
        for shift_z in range(3):
            base, todo, parts = 0, [], []
            for n, shift_x in enumerate(offsets(shift_z, sy)):
                slot = 0
                for rows in segments(shift_x):
                    patch_sums(
                        rows,
                        row,
                        lambda x, parity: moved(sy, x + shift_x, shift_z, parity),
                        lambda x, parity: below(sy, x + shift_x, (shift_z - 1) * (1 + parity)) if shift_z else 0.0,
                        parts,
                    )
                    todo.append((shift_x, rows, base, n, slot))
                    base += 16 * rows[1]
                    slot += rows[1]
            sums = jnp.dot(jnp.concatenate(parts, 0), band, preferred_element_type=F)
            for shift_x, rows, at, n, slot in todo:
                for j in range(rows[1]):
                    x = rows[0] + j
                    for parity in range(2):
                        distance = sums[at + 16 * j + 8 * parity : at + 16 * j + 8 * parity + 8]
                        weight = jnp.exp2(distance * rates[parity])
                        if x < 0 or x + shift_x < 0:
                            weight = weight * masks[0]
                        if x >= nx or x + shift_x >= nx:
                            weight = weight * masks[1]
                        if column_mask is not None:
                            weight = weight * column_mask[sy]
                        spot = (sy % 2, shift_z * 5 + n, slot + j, parity)
                        kept[spot] = weight
                        place[shift_z, shift_x, x, parity] = spot
        for x in range(nx):
            gather(sy, x, place, row, moved, kept, carry.at[sy % 2, x], last_slice, weighted, totals)


def plus(a, b):
    return b if a is None else a if b is None else a + b


def gather(sy, x, place, row, moved, kept, carry, last_slice, weighted, totals):
    ahead = [[None, None], [None, None]]
    back = [[[None, None] for _ in range(3)] for _ in range(2)]
    for shift_z in range(3):
        count = [None, None]
        for shift_x in offsets(shift_z, sy):
            for parity in range(2):
                spot = place.get((shift_z, shift_x, x, parity))
                if spot is not None:
                    weight = kept[spot]
                    ahead[0][parity] = plus(ahead[0][parity], weight * moved(sy, x + shift_x, shift_z, parity))
                    count[parity] = plus(count[parity], weight)
                spot = place.get((shift_z, shift_x, x - shift_x, parity))
                if spot is not None:
                    weight = kept[spot]
                    back[0][shift_z][parity] = plus(back[0][shift_z][parity], weight * row(x - shift_x, parity))
                    back[1][shift_z][parity] = plus(back[1][shift_z][parity], weight)
        for parity in range(2):
            if shift_z + parity >= 2 and count[parity] is not None:
                count[parity] = jnp.where(last_slice, 0.0, count[parity])
            ahead[1][parity] = plus(ahead[1][parity], count[parity])
    for m, total in enumerate((weighted, totals)):
        here = [plus(back[m][0][0], None), plus(back[m][0][1], back[m][1][0])]
        for parity, up in enumerate((plus(back[m][1][1], back[m][2][0]), back[m][2][1])):
            if up is not None:
                carry[2 * m + parity, 8:16] = up
                here[parity] = plus(here[parity], carry[2 * m + parity, 7:15])
        for parity in range(2):
            term = ahead[m][parity]
            if here[parity] is not None:
                term = plus(term, lane_roll(here[parity], sy - 2))
            if term is not None:
                total[x, parity] = total[x, parity] + term


def work(nx, rows):
    return [
        pltpu.VMEM((2, 15, rows, 2, 8, 128), F),
        pltpu.VMEM((2, nx, 4, 16, 128), F),
    ]


def inner_segments(shift_x):
    return ((2 + max(0, -shift_x), 12 - abs(shift_x)),)


def outer_segments(shift_x):
    many = 2 + abs(shift_x)
    return ((-max(0, shift_x), many), (14 - max(0, shift_x), many))


def whole_segments(nx):
    return lambda shift_x: ((-max(0, shift_x), nx + abs(shift_x)),)


def to_strips(value, chunk):
    lane = lanes() - 32 * chunk
    right = jnp.where((lane >= 16) & (lane < 24), lane_roll(value, 24 + 32 * chunk), 0.0)
    return jnp.where((lane >= 4) & (lane < 12), lane_roll(value, 4 + 32 * chunk), right)


def inner_kernel(noisy_ref, slices_ref, own_ref, rate_ref, copies, weighted, totals, rim_ref, left_ref, right_ref, steps, below, *scratch):
    def row(x, parity):
        return own_ref[x, parity]

    flat = noisy_ref.reshape(256, 128)
    for x in range(16):
        for parity in range(2):
            own_ref[x, parity] = flat[pl.ds(parity * 16 + x, 8, stride=32)]
    fill_copies(copies, steps, 16, row)
    fill_below(below, range(2, 14), row)
    lane = lanes()
    place = (lane % 32) // 4
    for x in range(12):
        for parity in range(2):
            value = jnp.zeros((8, 128), F)
            for chunk in range(4):
                source = 4 * chunk + x - HALO
                if 0 <= source < 16:
                    value = value + to_strips(own_ref[source, parity], chunk)
            rim_ref[x, parity] = value
    for group in range(3):
        for ref, column in ((left_ref, 0), (right_ref, 124)):
            message = jnp.zeros((8, 128), F)
            for chunk in range(4):
                for slot in range(8):
                    source = 4 * chunk + 4 * group + slot // 2 - HALO
                    if 0 <= source < 16:
                        here = (place == slot) & (lane // 32 == chunk)
                        message = jnp.where(here, lane_roll(own_ref[source, slot % 2], 32 * chunk + 4 * slot - column), message)
            ref[group] = message
    slices = jnp.broadcast_to(slices_ref[...], (8, 16))
    sublane, lane = [lax.broadcasted_iota(jnp.int32, (8, 16), dim) for dim in range(2)]
    for parity in range(2):
        rate = jnp.sum(jnp.where(lane == 2 * sublane + parity, slices, 0.0), axis=1, keepdims=True)
        rate_ref[parity] = jnp.broadcast_to(rate, (8, 128))

    one = jnp.ones((8, 128), F)
    accumulate(
        16,
        inner_segments,
        row,
        lambda sy, x, shift_z, parity: moved_row(copies, sy, x, shift_z, parity),
        lambda sy, x, j: below[sy, x - 2, j],
        (rate_ref[0], rate_ref[1]),
        None,
        None,
        lambda x, parity: (own_ref[x, parity], one),
        (*scratch, weighted, totals),
    )


def join_kernel(pair_ref, next_ref, rim_ref, left_ref, right_ref, low_ref, high_ref, rim_out, first_out, second_out):
    odd = flag("odd_x") > 0.5
    pair, other = pair_ref.reshape(256, 128), next_ref.reshape(256, 128)
    for x in range(HALO):
        for parity in range(2):
            line = pl.ds(parity * 16 + 12 + x, 8, stride=32)
            low_ref[x, parity] = jnp.where(odd, pair[line], other[line])
            line = pl.ds(parity * 16 + x, 8, stride=32)
            high_ref[x, parity] = jnp.where(odd, other[line], pair[line])
    lane = lanes()
    place = (lane % 32) // 4
    for x in range(12):
        for parity in range(2):
            value = rim_ref[x, parity]
            if x < HALO:
                value = value + to_strips(low_ref[x, parity], 0)
            if x >= 8:
                value = value + to_strips(high_ref[x - 8, parity], 3)
            rim_out[x, parity] = value
    messages = []
    for ref, column in ((left_ref, 0), (right_ref, 124)):
        groups = [ref[0], ref[1], ref[2]]
        for group, halo, chunk in ((0, low_ref, 0), (2, high_ref, 3)):
            for slot in range(8):
                here = (place == slot) & (lane // 32 == chunk)
                piece = lane_roll(halo[slot // 2, slot % 2], 32 * chunk + 4 * slot - column)
                groups[group] = jnp.where(here, piece, groups[group])
        messages.append(groups)
    odd = flag("odd_y") > 0.5
    for group in range(3):
        left, right = messages[0][group], messages[1][group]
        first_out[group] = jnp.where(odd, left, right)
        second_out[group] = jnp.where(odd, right, left)


def outer_kernel(own_ref, low_ref, high_ref, copies, rate_ref, inner_w, inner_t, mid_ref, far, steps, below, *scratch):
    def row(x, parity):
        if x < 0:
            return low_ref[x + HALO, parity]
        return own_ref[x, parity] if x < 16 else high_ref[x - 16, parity]

    def moved(sy, x, shift_z, parity):
        if 0 <= x < 16:
            return moved_row(copies, sy, x, shift_z, parity)
        return moved_row(far, sy, x + HALO if x < 0 else x - 12, shift_z, parity)

    def taken(sy, x, j):
        return below[sy, x + 2 if x < 6 else x - 2, j]

    fill_copies(far, steps, 8, lambda x, parity: row(x - HALO if x < HALO else x + 12, parity))
    fill_below(below, [*range(-2, 6), *range(10, 18)], row)
    one = jnp.ones((8, 128), F)
    accumulate(
        16,
        outer_segments,
        row,
        moved,
        taken,
        (rate_ref[0], rate_ref[1]),
        (flag("below"), flag("above")),
        None,
        lambda x, parity: (inner_w[x, parity], inner_t[x, parity]),
        scratch,
    )
    for x in range(16):
        for parity in range(2):
            mid_ref[x, parity] = scratch[-2][x, parity] / scratch[-1][x, parity]


def rim_kernel(rim_ref, first_ref, second_ref, rate_ref, mid_ref, out_ref, rows, copies, steps, below, column_mask, *scratch):
    lane = lanes()
    spot = lane % 32
    odd = flag("odd_y") > 0.5
    sides = [(first_ref[group], second_ref[group]) for group in range(3)]
    lefts = [jnp.where(odd, a, b) for a, b in sides]
    rights = [jnp.where(odd, b, a) for a, b in sides]
    for x in range(12):
        group, slot = x // 4, (x % 4) * 2
        for parity in range(2):
            value = rim_ref[x, parity]
            value = jnp.where(spot < 4, lane_roll(lefts[group], -4 * (slot + parity)), value)
            rows[x, parity] = jnp.where((spot >= 24) & (spot < 28), lane_roll(rights[group], 24 - 4 * (slot + parity)), value)
    for sy in range(5):
        off_left = (spot < 4) | ((spot + sy - 2 < 4) & (spot < 16))
        c = spot - 16
        off_right = (c >= 8) | ((c + sy - 2 >= 8) & (c >= 0))
        column_mask[sy] = jnp.where(off_left, flag("left"), 1.0) * jnp.where(off_right, flag("right"), 1.0)

    def row(x, parity):
        return rows[x + HALO, parity]

    fill_copies(copies, steps, 12, lambda x, parity: rows[x, parity])
    fill_below(below, range(-2, 6), row)
    one = jnp.ones((8, 128), F)
    accumulate(
        4,
        whole_segments(4),
        row,
        lambda sy, x, shift_z, parity: moved_row(copies, sy, x + HALO, shift_z, parity),
        lambda sy, x, j: below[sy, x + 2, j],
        (rate_ref[0], rate_ref[1]),
        (jnp.where(lane < 32, flag("below"), 1.0), jnp.where(lane >= 96, flag("above"), 1.0)),
        column_mask,
        lambda x, parity: (rows[x + HALO, parity], one),
        scratch,
    )
    flat = out_ref.reshape(256, 128)
    for x in range(4):
        for parity in range(2):
            value = scratch[-2][x, parity] / scratch[-1][x, parity]
            for chunk in range(4):
                at = 4 * chunk + x
                edge = jnp.where(lane < 4, lane_roll(value, -32 * chunk - 4), lane_roll(value, 104 - 32 * chunk))
                flat[pl.ds(parity * 16 + at, 8, stride=32)] = jnp.where((lane < 4) | (lane >= 124), edge, mid_ref[at, parity])


def flag(what):
    gx, gy = lax.axis_index("gx"), lax.axis_index("gy")
    holds = {
        "below": gx > 0,
        "above": gx < lax.axis_size("gx") - 1,
        "left": gy > 0,
        "right": gy < lax.axis_size("gy") - 1,
        "odd_x": gx % 2 == 1,
        "odd_y": gy % 2 == 1,
    }
    return jnp.full((8, 128), jnp.where(holds[what], 1.0, 0.0), F)


def shape(*dims):
    return jax.ShapeDtypeStruct(dims, F)


def call(kernel, name, outs, scratch, mib, flops=0):
    spec = pl.BlockSpec(memory_space=pltpu.VMEM)
    return pl.pallas_call(
        kernel,
        out_shape=outs,
        out_specs=jax.tree.map(lambda _: spec, outs),
        in_specs=INPUTS[name] * [spec],
        scratch_shapes=scratch,
        compiler_params=pltpu.CompilerParams(vmem_limit_bytes=mib * 2**20),
        cost_estimate=pl.CostEstimate(flops=flops, bytes_accessed=500_000, transcendentals=0),
        name=name,
    )


INPUTS = {"inner": 2, "join": 5, "outer": 7, "rim": 5}


def swapped(value, axis, first):
    pairs = [(a, a + 1) for a in range(first, lax.axis_size(axis) - 1, 2)]
    return lax.ppermute(value, axis, pairs + [(b, a) for a, b in pairs])


def per_device(noisy, strength):
    V = pltpu.VMEM
    row4, row12, row16, three = shape(4, 2, 8, 128), shape(12, 2, 8, 128), shape(16, 2, 8, 128), shape(3, 8, 128)
    rates = ((-math.log2(math.e) / 125.0) / strength).reshape(1, 16)
    pair = swapped(noisy, "gx", 0)
    other = swapped(noisy, "gx", 1)
    own, rate, copies, inner_w, inner_t, rim, to_left, to_right = call(
        inner_kernel,
        "inner",
        (row16, shape(2, 8, 128), shape(5, 16, 5, 8, 128), row16, row16, row12, three, three),
        [V((16, 2, 16, 128), F), V((5, 12, 3, 8, 128), F)] + work(16, 16),
        20,
        60_000_000,
    )(noisy, rates)
    low, high, rim, first, second = call(join_kernel, "join", (row4, row4, row12, three, three), [], 4)(
        pair, other, rim, to_left, to_right
    )
    first = swapped(first, "gy", 0)
    second = swapped(second, "gy", 1)
    mid = call(
        outer_kernel,
        "outer",
        row16,
        [V((5, 8, 5, 8, 128), F), V((8, 2, 16, 128), F), V((5, 16, 3, 8, 128), F)]
        + work(16, 8)
        + [V((16, 2, 8, 128), F)] * 2,
        20,
        40_000_000,
    )(own, low, high, copies, rate, inner_w, inner_t)
    return call(
        rim_kernel,
        "rim",
        shape(16, 16, 128),
        [V((12, 2, 8, 128), F), V((5, 12, 5, 8, 128), F), V((12, 2, 16, 128), F), V((5, 8, 3, 8, 128), F), V((5, 8, 128), F)]
        + work(4, 8)
        + [V((4, 2, 8, 128), F)] * 2,
        20,
        20_000_000,
    )(rim, first, second, rate, mid)


def solution(mesh):
    placed = (P(None, "gx", "gy"), P())
    return jax.shard_map(per_device, mesh=mesh, in_specs=placed, out_specs=P(None, "gx", "gy"), check_vma=False)
```

```python
import math

import jax
import jax.numpy as jnp
from jax import lax
from jax.experimental import pallas as pl
from jax.experimental.pallas import tpu as pltpu
from jax.sharding import PartitionSpec as P

F = jnp.float32
B = jnp.bfloat16
HALO = 4
SPLIT = 3


def lanes():
    return lax.broadcasted_iota(jnp.int32, (8, 128), 1)


def lane_roll(value, steps):
    steps %= 128
    return pltpu.roll(value, steps, 1) if steps else value


def offsets(shift_z, sy):
    if shift_z:
        return (-2, -1, 0, 1, 2)
    return (0, 1, 2) if sy > 2 else (1, 2)


def moved_row(copies, sy, row, shift_z, parity):
    return copies[sy, row, shift_z + parity]


def fill_copies(copies, steps, count, row):
    flat = steps.reshape(2 * count * 16, 128)
    for slot in range(0, 2 * count, 8):
        flat[pl.ds(16 * slot + 8, 8, stride=16)] = jnp.zeros((8, 128), F)
    for x in range(count):
        for parity in range(2):
            value = row(x, parity)
            steps[x, parity, 0:8] = value
            up = steps[x, parity, 1:9]
            for sy in range(5):
                copies[sy, x, parity] = lane_roll(value, 2 - sy)
                copies[sy, x, parity + 2] = lane_roll(up, 2 - sy)


def fill_below(below, centers, row):
    squares = {}

    def square(x):
        if x not in squares:
            squares[x] = [row(x, parity) * row(x, parity) for parity in range(2)]
        return squares[x]

    for place, x in enumerate(centers):
        sums = []
        for parity in range(2):
            near = square(x - 1)[parity] + square(x + 1)[parity]
            far = square(x - 2)[parity] + square(x + 2)[parity]
            sums.append(square(x)[parity] + near + far)
        three = (sums[0], sums[0] + sums[1], sums[1])
        for j in range(3):
            for sy in range(5):
                below[sy, place, j] = lane_roll(three[j], 2 - sy)


def patch_sums(rows, row, moved, under, parts):
    first, count = rows
    sub = lax.broadcasted_iota(jnp.int32, (8, 128), 0)
    top, bottom = sub == 0, sub == 7
    squared, pairs, fours = {}, {}, {}

    def square(m):
        if m not in squared:
            x = first - 2 + m
            differences = [row(x, parity) - moved(x, parity) for parity in range(2)]
            squared[m] = [d * d for d in differences]
        return squared[m]

    def pair(m):
        if m not in pairs:
            pairs[m] = [a + b for a, b in zip(square(m), square(m + 1))]
        return pairs[m]

    def four(m):
        if m not in fours:
            fours[m] = [a + b for a, b in zip(pair(m), pair(m + 2))]
        return fours[m]

    for j in range(count):
        shared, other = (four(j + 1), square(j)) if j % 2 == 0 else (four(j), square(j + 4))
        even, odd = [a + b for a, b in zip(shared, other)]
        both = even + odd
        up = jnp.where(top, under(first + j, 0), pltpu.roll(both, 1, 0))
        down = jnp.where(bottom, 0.0, pltpu.roll(both, 7, 0))
        even, odd = (
            both + up + jnp.where(bottom, 0.0, pltpu.roll(even, 7, 0)),
            both + down + jnp.where(top, under(first + j, 1), pltpu.roll(odd, 1, 0)),
        )
        sums = jnp.concatenate([even, odd], 0)
        high = sums.astype(B)
        parts.append(jnp.concatenate([high, (sums - high.astype(F)).astype(B)], 1))


def accumulate(nx, segments, row, moved, below, rates, masks, column_mask, start, scratch):
    kept, carry, weighted, totals = scratch
    last_slice = lax.broadcasted_iota(jnp.int32, (8, 128), 0) == 7
    carry_flat = carry.reshape(2 * nx * 4 * 16, 128)
    for slot in range(0, 8 * nx, 8):
        carry_flat[pl.ds(16 * slot + 7, 8, stride=16)] = jnp.zeros((8, 128), F)
    for x in range(nx):
        for parity in range(2):
            weighted[x, parity], totals[x, parity] = start(x, parity)
    line = lax.broadcasted_iota(jnp.int32, (256, 128), 0) % 128
    column = lax.broadcasted_iota(jnp.int32, (256, 128), 1)
    band = jnp.where(abs(line - column) <= 2, 1.0, 0.0).astype(B)
    for sy in range(5):
        place = {}
        base, todo, parts = 0, [], []
        for shift_z in range(3):
            for n, shift_x in enumerate(offsets(shift_z, sy)):
                slot = 0
                for rows in segments(shift_x, sy):
                    patch_sums(
                        rows,
                        row,
                        lambda x, parity: moved(sy, x + shift_x, shift_z, parity),
                        lambda x, parity: below(sy, x + shift_x, (shift_z - 1) * (1 + parity)) if shift_z else 0.0,
                        parts,
                    )
                    todo.append((shift_z, shift_x, rows, base, n, slot))
                    base += 16 * rows[1]
                    slot += rows[1]
        if parts:
            sums = jnp.dot(jnp.concatenate(parts, 0), band, preferred_element_type=F)
            for shift_z, shift_x, rows, at, n, slot in todo:
                for j in range(rows[1]):
                    x = rows[0] + j
                    for parity in range(2):
                        distance = sums[at + 16 * j + 8 * parity : at + 16 * j + 8 * parity + 8]
                        weight = jnp.exp2(distance * rates[parity])
                        if x < 0 or x + shift_x < 0:
                            weight = weight * masks[0]
                        if x >= nx or x + shift_x >= nx:
                            weight = weight * masks[1]
                        if column_mask is not None:
                            weight = weight * column_mask[sy]
                        spot = (sy % 2, shift_z * 5 + n, slot + j, parity)
                        kept[spot] = weight
                        place[shift_z, shift_x, x, parity] = spot
        for x in range(nx):
            gather(sy, x, place, row, moved, kept, carry.at[sy % 2, x], last_slice, weighted, totals)


def plus(a, b):
    return b if a is None else a if b is None else a + b


def gather(sy, x, place, row, moved, kept, carry, last_slice, weighted, totals):
    ahead = [[None, None], [None, None]]
    back = [[[None, None] for _ in range(3)] for _ in range(2)]
    for shift_z in range(3):
        count = [None, None]
        for shift_x in offsets(shift_z, sy):
            for parity in range(2):
                spot = place.get((shift_z, shift_x, x, parity))
                if spot is not None:
                    weight = kept[spot]
                    ahead[0][parity] = plus(ahead[0][parity], weight * moved(sy, x + shift_x, shift_z, parity))
                    count[parity] = plus(count[parity], weight)
                spot = place.get((shift_z, shift_x, x - shift_x, parity))
                if spot is not None:
                    weight = kept[spot]
                    back[0][shift_z][parity] = plus(back[0][shift_z][parity], weight * row(x - shift_x, parity))
                    back[1][shift_z][parity] = plus(back[1][shift_z][parity], weight)
        for parity in range(2):
            if shift_z + parity >= 2 and count[parity] is not None:
                count[parity] = jnp.where(last_slice, 0.0, count[parity])
            ahead[1][parity] = plus(ahead[1][parity], count[parity])
    for m, total in enumerate((weighted, totals)):
        here = [plus(back[m][0][0], None), plus(back[m][0][1], back[m][1][0])]
        for parity, up in enumerate((plus(back[m][1][1], back[m][2][0]), back[m][2][1])):
            if up is not None:
                carry[2 * m + parity, 8:16] = up
                here[parity] = plus(here[parity], carry[2 * m + parity, 7:15])
        for parity in range(2):
            term = ahead[m][parity]
            if here[parity] is not None:
                term = plus(term, lane_roll(here[parity], sy - 2))
            if term is not None:
                total[x, parity] = total[x, parity] + term


def work(nx, rows):
    return [
        pltpu.VMEM((2, 15, rows, 2, 8, 128), F),
        pltpu.VMEM((2, nx, 4, 16, 128), F),
    ]


def inner_segments(shift_x, sy):
    if sy >= SPLIT:
        return ()
    return ((2 + max(0, -shift_x), 12 - abs(shift_x)),)


def outer_segments(shift_x, sy):
    if sy >= SPLIT:
        return ((-max(0, shift_x), 16 + abs(shift_x)),)
    many = 2 + abs(shift_x)
    return ((-max(0, shift_x), many), (14 - max(0, shift_x), many))


def whole_segments(nx):
    return lambda shift_x, sy: ((-max(0, shift_x), nx + abs(shift_x)),)


def to_strips(value, chunk):
    lane = lanes() - 32 * chunk
    right = jnp.where((lane >= 16) & (lane < 24), lane_roll(value, 24 + 32 * chunk), 0.0)
    return jnp.where((lane >= 4) & (lane < 12), lane_roll(value, 4 + 32 * chunk), right)


def inner_kernel(noisy_ref, slices_ref, own_ref, rate_ref, copies, weighted, totals, rim_ref, left_ref, right_ref, steps, below, *scratch):
    def row(x, parity):
        return own_ref[x, parity]

    flat = noisy_ref.reshape(256, 128)
    for x in range(16):
        for parity in range(2):
            own_ref[x, parity] = flat[pl.ds(parity * 16 + x, 8, stride=32)]
    fill_copies(copies, steps, 16, row)
    fill_below(below, range(2, 14), row)
    lane = lanes()
    place = (lane % 32) // 4
    for x in range(12):
        for parity in range(2):
            value = jnp.zeros((8, 128), F)
            for chunk in range(4):
                source = 4 * chunk + x - HALO
                if 0 <= source < 16:
                    value = value + to_strips(own_ref[source, parity], chunk)
            rim_ref[x, parity] = value
    for group in range(3):
        for ref, column in ((left_ref, 0), (right_ref, 124)):
            message = jnp.zeros((8, 128), F)
            for chunk in range(4):
                for slot in range(8):
                    source = 4 * chunk + 4 * group + slot // 2 - HALO
                    if 0 <= source < 16:
                        here = (place == slot) & (lane // 32 == chunk)
                        message = jnp.where(here, lane_roll(own_ref[source, slot % 2], 32 * chunk + 4 * slot - column), message)
            ref[group] = message
    slices = jnp.broadcast_to(slices_ref[...], (8, 16))
    sublane, lane = [lax.broadcasted_iota(jnp.int32, (8, 16), dim) for dim in range(2)]
    for parity in range(2):
        rate = jnp.sum(jnp.where(lane == 2 * sublane + parity, slices, 0.0), axis=1, keepdims=True)
        rate_ref[parity] = jnp.broadcast_to(rate, (8, 128))

    one = jnp.ones((8, 128), F)
    accumulate(
        16,
        inner_segments,
        row,
        lambda sy, x, shift_z, parity: moved_row(copies, sy, x, shift_z, parity),
        lambda sy, x, j: below[sy, x - 2, j],
        (rate_ref[0], rate_ref[1]),
        None,
        None,
        lambda x, parity: (own_ref[x, parity], one),
        (*scratch, weighted, totals),
    )


def join_kernel(pair_ref, next_ref, rim_ref, left_ref, right_ref, low_ref, high_ref, rim_out, first_out, second_out):
    odd = flag("odd_x") > 0.5
    pair, other = pair_ref.reshape(256, 128), next_ref.reshape(256, 128)
    for x in range(HALO):
        for parity in range(2):
            line = pl.ds(parity * 16 + 12 + x, 8, stride=32)
            low_ref[x, parity] = jnp.where(odd, pair[line], other[line])
            line = pl.ds(parity * 16 + x, 8, stride=32)
            high_ref[x, parity] = jnp.where(odd, other[line], pair[line])
    lane = lanes()
    place = (lane % 32) // 4
    for x in range(12):
        for parity in range(2):
            value = rim_ref[x, parity]
            if x < HALO:
                value = value + to_strips(low_ref[x, parity], 0)
            if x >= 8:
                value = value + to_strips(high_ref[x - 8, parity], 3)
            rim_out[x, parity] = value
    messages = []
    for ref, column in ((left_ref, 0), (right_ref, 124)):
        groups = [ref[0], ref[1], ref[2]]
        for group, halo, chunk in ((0, low_ref, 0), (2, high_ref, 3)):
            for slot in range(8):
                here = (place == slot) & (lane // 32 == chunk)
                piece = lane_roll(halo[slot // 2, slot % 2], 32 * chunk + 4 * slot - column)
                groups[group] = jnp.where(here, piece, groups[group])
        messages.append(groups)
    odd = flag("odd_y") > 0.5
    for group in range(3):
        left, right = messages[0][group], messages[1][group]
        first_out[group] = jnp.where(odd, left, right)
        second_out[group] = jnp.where(odd, right, left)


def outer_kernel(own_ref, low_ref, high_ref, copies, rate_ref, inner_w, inner_t, mid_ref, far, steps, below, *scratch):
    def row(x, parity):
        if x < 0:
            return low_ref[x + HALO, parity]
        return own_ref[x, parity] if x < 16 else high_ref[x - 16, parity]

    def moved(sy, x, shift_z, parity):
        if 0 <= x < 16:
            return moved_row(copies, sy, x, shift_z, parity)
        return moved_row(far, sy, x + HALO if x < 0 else x - 12, shift_z, parity)

    def taken(sy, x, j):
        return below[sy, x + 2, j]

    fill_copies(far, steps, 8, lambda x, parity: row(x - HALO if x < HALO else x + 12, parity))
    fill_below(below, range(-2, 18), row)
    one = jnp.ones((8, 128), F)
    accumulate(
        16,
        outer_segments,
        row,
        moved,
        taken,
        (rate_ref[0], rate_ref[1]),
        (flag("below"), flag("above")),
        None,
        lambda x, parity: (inner_w[x, parity], inner_t[x, parity]),
        scratch,
    )
    for x in range(16):
        for parity in range(2):
            mid_ref[x, parity] = scratch[-2][x, parity] / scratch[-1][x, parity]


def rim_kernel(rim_ref, first_ref, second_ref, rate_ref, mid_ref, out_ref, rows, copies, steps, below, column_mask, *scratch):
    lane = lanes()
    spot = lane % 32
    odd = flag("odd_y") > 0.5
    sides = [(first_ref[group], second_ref[group]) for group in range(3)]
    lefts = [jnp.where(odd, a, b) for a, b in sides]
    rights = [jnp.where(odd, b, a) for a, b in sides]
    for x in range(12):
        group, slot = x // 4, (x % 4) * 2
        for parity in range(2):
            value = rim_ref[x, parity]
            value = jnp.where(spot < 4, lane_roll(lefts[group], -4 * (slot + parity)), value)
            rows[x, parity] = jnp.where((spot >= 24) & (spot < 28), lane_roll(rights[group], 24 - 4 * (slot + parity)), value)
    for sy in range(5):
        off_left = (spot < 4) | ((spot + sy - 2 < 4) & (spot < 16))
        c = spot - 16
        off_right = (c >= 8) | ((c + sy - 2 >= 8) & (c >= 0))
        column_mask[sy] = jnp.where(off_left, flag("left"), 1.0) * jnp.where(off_right, flag("right"), 1.0)

    def row(x, parity):
        return rows[x + HALO, parity]

    fill_copies(copies, steps, 12, lambda x, parity: rows[x, parity])
    fill_below(below, range(-2, 6), row)
    one = jnp.ones((8, 128), F)
    accumulate(
        4,
        whole_segments(4),
        row,
        lambda sy, x, shift_z, parity: moved_row(copies, sy, x + HALO, shift_z, parity),
        lambda sy, x, j: below[sy, x + 2, j],
        (rate_ref[0], rate_ref[1]),
        (jnp.where(lane < 32, flag("below"), 1.0), jnp.where(lane >= 96, flag("above"), 1.0)),
        column_mask,
        lambda x, parity: (rows[x + HALO, parity], one),
        scratch,
    )
    flat = out_ref.reshape(256, 128)
    for x in range(4):
        for parity in range(2):
            value = scratch[-2][x, parity] / scratch[-1][x, parity]
            for chunk in range(4):
                at = 4 * chunk + x
                edge = jnp.where(lane < 4, lane_roll(value, -32 * chunk - 4), lane_roll(value, 104 - 32 * chunk))
                flat[pl.ds(parity * 16 + at, 8, stride=32)] = jnp.where((lane < 4) | (lane >= 124), edge, mid_ref[at, parity])


def flag(what):
    gx, gy = lax.axis_index("gx"), lax.axis_index("gy")
    holds = {
        "below": gx > 0,
        "above": gx < lax.axis_size("gx") - 1,
        "left": gy > 0,
        "right": gy < lax.axis_size("gy") - 1,
        "odd_x": gx % 2 == 1,
        "odd_y": gy % 2 == 1,
    }
    return jnp.full((8, 128), jnp.where(holds[what], 1.0, 0.0), F)


def shape(*dims):
    return jax.ShapeDtypeStruct(dims, F)


def call(kernel, name, outs, scratch, mib, flops=0):
    spec = pl.BlockSpec(memory_space=pltpu.VMEM)
    return pl.pallas_call(
        kernel,
        out_shape=outs,
        out_specs=jax.tree.map(lambda _: spec, outs),
        in_specs=INPUTS[name] * [spec],
        scratch_shapes=scratch,
        compiler_params=pltpu.CompilerParams(vmem_limit_bytes=mib * 2**20),
        cost_estimate=pl.CostEstimate(flops=flops, bytes_accessed=500_000, transcendentals=0),
        name=name,
    )


INPUTS = {"inner": 2, "join": 5, "outer": 7, "rim": 5}


def swapped(value, axis, first):
    pairs = [(a, a + 1) for a in range(first, lax.axis_size(axis) - 1, 2)]
    return lax.ppermute(value, axis, pairs + [(b, a) for a, b in pairs])


def per_device(noisy, strength):
    V = pltpu.VMEM
    row4, row12, row16, three = shape(4, 2, 8, 128), shape(12, 2, 8, 128), shape(16, 2, 8, 128), shape(3, 8, 128)
    rates = ((-math.log2(math.e) / 125.0) / strength).reshape(1, 16)
    other = swapped(noisy, "gx", 1)
    pair = swapped(noisy, "gx", 0)
    own, rate, copies, inner_w, inner_t, rim, to_left, to_right = call(
        inner_kernel,
        "inner",
        (row16, shape(2, 8, 128), shape(5, 16, 5, 8, 128), row16, row16, row12, three, three),
        [V((16, 2, 16, 128), F), V((5, 12, 3, 8, 128), F)] + work(16, 16),
        20,
        60_000_000,
    )(noisy, rates)
    low, high, rim, first, second = call(join_kernel, "join", (row4, row4, row12, three, three), [], 4)(
        pair, other, rim, to_left, to_right
    )
    second = swapped(second, "gy", 1)
    first = swapped(first, "gy", 0)
    mid = call(
        outer_kernel,
        "outer",
        row16,
        [V((5, 8, 5, 8, 128), F), V((8, 2, 16, 128), F), V((5, 20, 3, 8, 128), F)]
        + work(16, 18)
        + [V((16, 2, 8, 128), F)] * 2,
        20,
        40_000_000,
    )(own, low, high, copies, rate, inner_w, inner_t)
    return call(
        rim_kernel,
        "rim",
        shape(16, 16, 128),
        [V((12, 2, 8, 128), F), V((5, 12, 5, 8, 128), F), V((12, 2, 16, 128), F), V((5, 8, 3, 8, 128), F), V((5, 8, 128), F)]
        + work(4, 8)
        + [V((4, 2, 8, 128), F)] * 2,
        20,
        20_000_000,
    )(rim, first, second, rate, mid)


def solution(mesh):
    placed = (P(None, "gx", "gy"), P())
    return jax.shard_map(per_device, mesh=mesh, in_specs=placed, out_specs=P(None, "gx", "gy"), check_vma=False)
```

```python
import math

import jax
import jax.numpy as jnp
from jax import lax
from jax.experimental import pallas as pl
from jax.experimental.pallas import tpu as pltpu
from jax.sharding import PartitionSpec as P

F = jnp.float32
B = jnp.bfloat16
HALO = 4
SPLIT = 4


def lanes():
    return lax.broadcasted_iota(jnp.int32, (8, 128), 1)


def lane_roll(value, steps):
    steps %= 128
    return pltpu.roll(value, steps, 1) if steps else value


def offsets(shift_z, sy):
    if shift_z:
        return (-2, -1, 0, 1, 2)
    return (0, 1, 2) if sy > 2 else (1, 2)


def moved_row(copies, sy, row, shift_z, parity):
    return copies[sy, row, shift_z + parity]


def fill_copies(copies, steps, count, row):
    flat = steps.reshape(2 * count * 16, 128)
    for slot in range(0, 2 * count, 8):
        flat[pl.ds(16 * slot + 8, 8, stride=16)] = jnp.zeros((8, 128), F)
    for x in range(count):
        for parity in range(2):
            value = row(x, parity)
            steps[x, parity, 0:8] = value
            up = steps[x, parity, 1:9]
            for sy in range(5):
                copies[sy, x, parity] = lane_roll(value, 2 - sy)
                copies[sy, x, parity + 2] = lane_roll(up, 2 - sy)


def fill_below(below, centers, row):
    squares = {}

    def square(x):
        if x not in squares:
            squares[x] = [row(x, parity) * row(x, parity) for parity in range(2)]
        return squares[x]

    for place, x in enumerate(centers):
        sums = []
        for parity in range(2):
            near = square(x - 1)[parity] + square(x + 1)[parity]
            far = square(x - 2)[parity] + square(x + 2)[parity]
            sums.append(square(x)[parity] + near + far)
        three = (sums[0], sums[0] + sums[1], sums[1])
        for j in range(3):
            for sy in range(5):
                below[sy, place, j] = lane_roll(three[j], 2 - sy)


def patch_sums(rows, row, moved, under, parts):
    first, count = rows
    sub = lax.broadcasted_iota(jnp.int32, (8, 128), 0)
    top, bottom = sub == 0, sub == 7
    squared, pairs, fours = {}, {}, {}

    def square(m):
        if m not in squared:
            x = first - 2 + m
            differences = [row(x, parity) - moved(x, parity) for parity in range(2)]
            squared[m] = [d * d for d in differences]
        return squared[m]

    def pair(m):
        if m not in pairs:
            pairs[m] = [a + b for a, b in zip(square(m), square(m + 1))]
        return pairs[m]

    def four(m):
        if m not in fours:
            fours[m] = [a + b for a, b in zip(pair(m), pair(m + 2))]
        return fours[m]

    for j in range(count):
        shared, other = (four(j + 1), square(j)) if j % 2 == 0 else (four(j), square(j + 4))
        even, odd = [a + b for a, b in zip(shared, other)]
        both = even + odd
        up = jnp.where(top, under(first + j, 0), pltpu.roll(both, 1, 0))
        down = jnp.where(bottom, 0.0, pltpu.roll(both, 7, 0))
        even, odd = (
            both + up + jnp.where(bottom, 0.0, pltpu.roll(even, 7, 0)),
            both + down + jnp.where(top, under(first + j, 1), pltpu.roll(odd, 1, 0)),
        )
        sums = jnp.concatenate([even, odd], 0)
        high = sums.astype(B)
        parts.append(jnp.concatenate([high, (sums - high.astype(F)).astype(B)], 1))


def accumulate(nx, segments, row, moved, below, rates, masks, column_mask, start, scratch):
    kept, carry, weighted, totals = scratch
    last_slice = lax.broadcasted_iota(jnp.int32, (8, 128), 0) == 7
    carry_flat = carry.reshape(2 * nx * 4 * 16, 128)
    for slot in range(0, 8 * nx, 8):
        carry_flat[pl.ds(16 * slot + 7, 8, stride=16)] = jnp.zeros((8, 128), F)
    for x in range(nx):
        for parity in range(2):
            weighted[x, parity], totals[x, parity] = start(x, parity)
    line = lax.broadcasted_iota(jnp.int32, (256, 128), 0) % 128
    column = lax.broadcasted_iota(jnp.int32, (256, 128), 1)
    band = jnp.where(abs(line - column) <= 2, 1.0, 0.0).astype(B)
    for sy in range(5):
        place = {}
        base, todo, parts = 0, [], []
        for shift_z in range(3):
            for n, shift_x in enumerate(offsets(shift_z, sy)):
                slot = 0
                for rows in segments(shift_x, sy):
                    patch_sums(
                        rows,
                        row,
                        lambda x, parity: moved(sy, x + shift_x, shift_z, parity),
                        lambda x, parity: below(sy, x + shift_x, (shift_z - 1) * (1 + parity)) if shift_z else 0.0,
                        parts,
                    )
                    todo.append((shift_z, shift_x, rows, base, n, slot))
                    base += 16 * rows[1]
                    slot += rows[1]
        if parts:
            sums = jnp.dot(jnp.concatenate(parts, 0), band, preferred_element_type=F)
            for shift_z, shift_x, rows, at, n, slot in todo:
                for j in range(rows[1]):
                    x = rows[0] + j
                    for parity in range(2):
                        distance = sums[at + 16 * j + 8 * parity : at + 16 * j + 8 * parity + 8]
                        weight = jnp.exp2(distance * rates[parity])
                        if x < 0 or x + shift_x < 0:
                            weight = weight * masks[0]
                        if x >= nx or x + shift_x >= nx:
                            weight = weight * masks[1]
                        if column_mask is not None:
                            weight = weight * column_mask[sy]
                        spot = (sy % 2, shift_z * 5 + n, slot + j, parity)
                        kept[spot] = weight
                        place[shift_z, shift_x, x, parity] = spot
        for x in range(nx):
            gather(sy, x, place, row, moved, kept, carry.at[sy % 2, x], last_slice, weighted, totals)


def plus(a, b):
    return b if a is None else a if b is None else a + b


def gather(sy, x, place, row, moved, kept, carry, last_slice, weighted, totals):
    ahead = [[None, None], [None, None]]
    back = [[[None, None] for _ in range(3)] for _ in range(2)]
    for shift_z in range(3):
        count = [None, None]
        for shift_x in offsets(shift_z, sy):
            for parity in range(2):
                spot = place.get((shift_z, shift_x, x, parity))
                if spot is not None:
                    weight = kept[spot]
                    ahead[0][parity] = plus(ahead[0][parity], weight * moved(sy, x + shift_x, shift_z, parity))
                    count[parity] = plus(count[parity], weight)
                spot = place.get((shift_z, shift_x, x - shift_x, parity))
                if spot is not None:
                    weight = kept[spot]
                    back[0][shift_z][parity] = plus(back[0][shift_z][parity], weight * row(x - shift_x, parity))
                    back[1][shift_z][parity] = plus(back[1][shift_z][parity], weight)
        for parity in range(2):
            if shift_z + parity >= 2 and count[parity] is not None:
                count[parity] = jnp.where(last_slice, 0.0, count[parity])
            ahead[1][parity] = plus(ahead[1][parity], count[parity])
    for m, total in enumerate((weighted, totals)):
        here = [plus(back[m][0][0], None), plus(back[m][0][1], back[m][1][0])]
        for parity, up in enumerate((plus(back[m][1][1], back[m][2][0]), back[m][2][1])):
            if up is not None:
                carry[2 * m + parity, 8:16] = up
                here[parity] = plus(here[parity], carry[2 * m + parity, 7:15])
        for parity in range(2):
            term = ahead[m][parity]
            if here[parity] is not None:
                term = plus(term, lane_roll(here[parity], sy - 2))
            if term is not None:
                total[x, parity] = total[x, parity] + term


def work(nx, rows):
    return [
        pltpu.VMEM((2, 15, rows, 2, 8, 128), F),
        pltpu.VMEM((2, nx, 4, 16, 128), F),
    ]


def inner_segments(shift_x, sy):
    if sy >= SPLIT:
        return ()
    return ((2 + max(0, -shift_x), 12 - abs(shift_x)),)


def outer_segments(shift_x, sy):
    if sy >= SPLIT:
        return ((-max(0, shift_x), 16 + abs(shift_x)),)
    many = 2 + abs(shift_x)
    return ((-max(0, shift_x), many), (14 - max(0, shift_x), many))


def whole_segments(nx):
    return lambda shift_x, sy: ((-max(0, shift_x), nx + abs(shift_x)),)


def to_strips(value, chunk):
    lane = lanes() - 32 * chunk
    right = jnp.where((lane >= 16) & (lane < 24), lane_roll(value, 24 + 32 * chunk), 0.0)
    return jnp.where((lane >= 4) & (lane < 12), lane_roll(value, 4 + 32 * chunk), right)


def inner_kernel(noisy_ref, slices_ref, own_ref, rate_ref, copies, weighted, totals, rim_ref, left_ref, right_ref, steps, below, *scratch):
    def row(x, parity):
        return own_ref[x, parity]

    flat = noisy_ref.reshape(256, 128)
    for x in range(16):
        for parity in range(2):
            own_ref[x, parity] = flat[pl.ds(parity * 16 + x, 8, stride=32)]
    fill_copies(copies, steps, 16, row)
    fill_below(below, range(2, 14), row)
    lane = lanes()
    place = (lane % 32) // 4
    for x in range(12):
        for parity in range(2):
            value = jnp.zeros((8, 128), F)
            for chunk in range(4):
                source = 4 * chunk + x - HALO
                if 0 <= source < 16:
                    value = value + to_strips(own_ref[source, parity], chunk)
            rim_ref[x, parity] = value
    for group in range(3):
        for ref, column in ((left_ref, 0), (right_ref, 124)):
            message = jnp.zeros((8, 128), F)
            for chunk in range(4):
                for slot in range(8):
                    source = 4 * chunk + 4 * group + slot // 2 - HALO
                    if 0 <= source < 16:
                        here = (place == slot) & (lane // 32 == chunk)
                        message = jnp.where(here, lane_roll(own_ref[source, slot % 2], 32 * chunk + 4 * slot - column), message)
            ref[group] = message
    slices = jnp.broadcast_to(slices_ref[...], (8, 16))
    sublane, lane = [lax.broadcasted_iota(jnp.int32, (8, 16), dim) for dim in range(2)]
    for parity in range(2):
        rate = jnp.sum(jnp.where(lane == 2 * sublane + parity, slices, 0.0), axis=1, keepdims=True)
        rate_ref[parity] = jnp.broadcast_to(rate, (8, 128))

    one = jnp.ones((8, 128), F)
    accumulate(
        16,
        inner_segments,
        row,
        lambda sy, x, shift_z, parity: moved_row(copies, sy, x, shift_z, parity),
        lambda sy, x, j: below[sy, x - 2, j],
        (rate_ref[0], rate_ref[1]),
        None,
        None,
        lambda x, parity: (own_ref[x, parity], one),
        (*scratch, weighted, totals),
    )


def join_kernel(next_ref, pair_ref, rim_ref, left_ref, right_ref, low_ref, high_ref, rim_out, first_out, second_out):
    odd = flag("odd_x") > 0.5
    pair, other = pair_ref.reshape(256, 128), next_ref.reshape(256, 128)
    for x in range(HALO):
        for parity in range(2):
            line = pl.ds(parity * 16 + 12 + x, 8, stride=32)
            low_ref[x, parity] = jnp.where(odd, pair[line], other[line])
            line = pl.ds(parity * 16 + x, 8, stride=32)
            high_ref[x, parity] = jnp.where(odd, other[line], pair[line])
    lane = lanes()
    place = (lane % 32) // 4
    for x in range(12):
        for parity in range(2):
            value = rim_ref[x, parity]
            if x < HALO:
                value = value + to_strips(low_ref[x, parity], 0)
            if x >= 8:
                value = value + to_strips(high_ref[x - 8, parity], 3)
            rim_out[x, parity] = value
    messages = []
    for ref, column in ((left_ref, 0), (right_ref, 124)):
        groups = [ref[0], ref[1], ref[2]]
        for group, halo, chunk in ((0, low_ref, 0), (2, high_ref, 3)):
            for slot in range(8):
                here = (place == slot) & (lane // 32 == chunk)
                piece = lane_roll(halo[slot // 2, slot % 2], 32 * chunk + 4 * slot - column)
                groups[group] = jnp.where(here, piece, groups[group])
        messages.append(groups)
    odd = flag("odd_y") > 0.5
    for group in range(3):
        left, right = messages[0][group], messages[1][group]
        first_out[group] = jnp.where(odd, left, right)
        second_out[group] = jnp.where(odd, right, left)


def outer_kernel(own_ref, low_ref, high_ref, copies, rate_ref, inner_w, inner_t, mid_ref, far, steps, below, *scratch):
    def row(x, parity):
        if x < 0:
            return low_ref[x + HALO, parity]
        return own_ref[x, parity] if x < 16 else high_ref[x - 16, parity]

    def moved(sy, x, shift_z, parity):
        if 0 <= x < 16:
            return moved_row(copies, sy, x, shift_z, parity)
        return moved_row(far, sy, x + HALO if x < 0 else x - 12, shift_z, parity)

    def taken(sy, x, j):
        return below[sy, x + 2, j]

    fill_copies(far, steps, 8, lambda x, parity: row(x - HALO if x < HALO else x + 12, parity))
    fill_below(below, range(-2, 18), row)
    one = jnp.ones((8, 128), F)
    accumulate(
        16,
        outer_segments,
        row,
        moved,
        taken,
        (rate_ref[0], rate_ref[1]),
        (flag("below"), flag("above")),
        None,
        lambda x, parity: (inner_w[x, parity], inner_t[x, parity]),
        scratch,
    )
    for x in range(16):
        for parity in range(2):
            mid_ref[x, parity] = scratch[-2][x, parity] / scratch[-1][x, parity]


def rim_kernel(rim_ref, second_ref, first_ref, rate_ref, mid_ref, out_ref, rows, copies, steps, below, column_mask, *scratch):
    lane = lanes()
    spot = lane % 32
    odd = flag("odd_y") > 0.5
    sides = [(first_ref[group], second_ref[group]) for group in range(3)]
    lefts = [jnp.where(odd, a, b) for a, b in sides]
    rights = [jnp.where(odd, b, a) for a, b in sides]
    for x in range(12):
        group, slot = x // 4, (x % 4) * 2
        for parity in range(2):
            value = rim_ref[x, parity]
            value = jnp.where(spot < 4, lane_roll(lefts[group], -4 * (slot + parity)), value)
            rows[x, parity] = jnp.where((spot >= 24) & (spot < 28), lane_roll(rights[group], 24 - 4 * (slot + parity)), value)
    for sy in range(5):
        off_left = (spot < 4) | ((spot + sy - 2 < 4) & (spot < 16))
        c = spot - 16
        off_right = (c >= 8) | ((c + sy - 2 >= 8) & (c >= 0))
        column_mask[sy] = jnp.where(off_left, flag("left"), 1.0) * jnp.where(off_right, flag("right"), 1.0)

    def row(x, parity):
        return rows[x + HALO, parity]

    fill_copies(copies, steps, 12, lambda x, parity: rows[x, parity])
    fill_below(below, range(-2, 6), row)
    one = jnp.ones((8, 128), F)
    accumulate(
        4,
        whole_segments(4),
        row,
        lambda sy, x, shift_z, parity: moved_row(copies, sy, x + HALO, shift_z, parity),
        lambda sy, x, j: below[sy, x + 2, j],
        (rate_ref[0], rate_ref[1]),
        (jnp.where(lane < 32, flag("below"), 1.0), jnp.where(lane >= 96, flag("above"), 1.0)),
        column_mask,
        lambda x, parity: (rows[x + HALO, parity], one),
        scratch,
    )
    flat = out_ref.reshape(256, 128)
    for x in range(4):
        for parity in range(2):
            value = scratch[-2][x, parity] / scratch[-1][x, parity]
            for chunk in range(4):
                at = 4 * chunk + x
                edge = jnp.where(lane < 4, lane_roll(value, -32 * chunk - 4), lane_roll(value, 104 - 32 * chunk))
                flat[pl.ds(parity * 16 + at, 8, stride=32)] = jnp.where((lane < 4) | (lane >= 124), edge, mid_ref[at, parity])


def flag(what):
    gx, gy = lax.axis_index("gx"), lax.axis_index("gy")
    holds = {
        "below": gx > 0,
        "above": gx < lax.axis_size("gx") - 1,
        "left": gy > 0,
        "right": gy < lax.axis_size("gy") - 1,
        "odd_x": gx % 2 == 1,
        "odd_y": gy % 2 == 1,
    }
    return jnp.full((8, 128), jnp.where(holds[what], 1.0, 0.0), F)


def shape(*dims):
    return jax.ShapeDtypeStruct(dims, F)


def call(kernel, name, outs, scratch, mib, flops=0):
    spec = pl.BlockSpec(memory_space=pltpu.VMEM)
    return pl.pallas_call(
        kernel,
        out_shape=outs,
        out_specs=jax.tree.map(lambda _: spec, outs),
        in_specs=INPUTS[name] * [spec],
        scratch_shapes=scratch,
        compiler_params=pltpu.CompilerParams(vmem_limit_bytes=mib * 2**20),
        cost_estimate=pl.CostEstimate(flops=flops, bytes_accessed=500_000, transcendentals=0),
        name=name,
    )


INPUTS = {"inner": 2, "join": 5, "outer": 7, "rim": 5}


def swapped(value, axis, first):
    pairs = [(a, a + 1) for a in range(first, lax.axis_size(axis) - 1, 2)]
    return lax.ppermute(value, axis, pairs + [(b, a) for a, b in pairs])


def per_device(noisy, strength):
    V = pltpu.VMEM
    row4, row12, row16, three = shape(4, 2, 8, 128), shape(12, 2, 8, 128), shape(16, 2, 8, 128), shape(3, 8, 128)
    rates = ((-math.log2(math.e) / 125.0) / strength).reshape(1, 16)
    other = swapped(noisy, "gx", 1)
    pair = swapped(noisy, "gx", 0)
    own, rate, copies, inner_w, inner_t, rim, to_left, to_right = call(
        inner_kernel,
        "inner",
        (row16, shape(2, 8, 128), shape(5, 16, 5, 8, 128), row16, row16, row12, three, three),
        [V((16, 2, 16, 128), F), V((5, 12, 3, 8, 128), F)] + work(16, 16),
        20,
        60_000_000,
    )(noisy, rates)
    low, high, rim, first, second = call(join_kernel, "join", (row4, row4, row12, three, three), [], 4)(
        other, pair, rim, to_left, to_right
    )
    second = swapped(second, "gy", 1)
    first = swapped(first, "gy", 0)
    mid = call(
        outer_kernel,
        "outer",
        row16,
        [V((5, 8, 5, 8, 128), F), V((8, 2, 16, 128), F), V((5, 20, 3, 8, 128), F)]
        + work(16, 18)
        + [V((16, 2, 8, 128), F)] * 2,
        20,
        40_000_000,
    )(own, low, high, copies, rate, inner_w, inner_t)
    return call(
        rim_kernel,
        "rim",
        shape(16, 16, 128),
        [V((12, 2, 8, 128), F), V((5, 12, 5, 8, 128), F), V((12, 2, 16, 128), F), V((5, 8, 3, 8, 128), F), V((5, 8, 128), F)]
        + work(4, 8)
        + [V((4, 2, 8, 128), F)] * 2,
        20,
        20_000_000,
    )(rim, second, first, rate, mid)


def solution(mesh):
    placed = (P(None, "gx", "gy"), P())
    return jax.shard_map(per_device, mesh=mesh, in_specs=placed, out_specs=P(None, "gx", "gy"), check_vma=False)
```

```python
import math

import jax
import jax.numpy as jnp
from jax import lax
from jax.experimental import pallas as pl
from jax.experimental.pallas import tpu as pltpu
from jax.sharding import PartitionSpec as P

F = jnp.float32
B = jnp.bfloat16
HALO = 4
SPLIT = 4


def lanes():
    return lax.broadcasted_iota(jnp.int32, (8, 128), 1)


def lane_roll(value, steps):
    steps %= 128
    return pltpu.roll(value, steps, 1) if steps else value


def offsets(shift_z, sy):
    if shift_z:
        return (-2, -1, 0, 1, 2)
    return (0, 1, 2) if sy > 2 else (1, 2)


def moved_row(copies, sy, row, shift_z, parity):
    return copies[sy, row, shift_z + parity]


def fill_copies(copies, steps, count, row):
    flat = steps.reshape(2 * count * 16, 128)
    for slot in range(0, 2 * count, 8):
        flat[pl.ds(16 * slot + 8, 8, stride=16)] = jnp.zeros((8, 128), F)
    for x in range(count):
        for parity in range(2):
            value = row(x, parity)
            steps[x, parity, 0:8] = value
            up = steps[x, parity, 1:9]
            for sy in range(5):
                copies[sy, x, parity] = lane_roll(value, 2 - sy)
                copies[sy, x, parity + 2] = lane_roll(up, 2 - sy)


def fill_below(below, centers, row):
    squares = {}

    def square(x):
        if x not in squares:
            squares[x] = [row(x, parity) * row(x, parity) for parity in range(2)]
        return squares[x]

    for place, x in enumerate(centers):
        sums = []
        for parity in range(2):
            near = square(x - 1)[parity] + square(x + 1)[parity]
            far = square(x - 2)[parity] + square(x + 2)[parity]
            sums.append(square(x)[parity] + near + far)
        three = (sums[0], sums[0] + sums[1], sums[1])
        for j in range(3):
            for sy in range(5):
                below[sy, place, j] = lane_roll(three[j], 2 - sy)


def patch_sums(rows, row, moved, under, parts):
    first, count = rows
    sub = lax.broadcasted_iota(jnp.int32, (8, 128), 0)
    top, bottom = sub == 0, sub == 7
    squared, pairs, fours = {}, {}, {}

    def square(m):
        if m not in squared:
            x = first - 2 + m
            differences = [row(x, parity) - moved(x, parity) for parity in range(2)]
            squared[m] = [d * d for d in differences]
        return squared[m]

    def pair(m):
        if m not in pairs:
            pairs[m] = [a + b for a, b in zip(square(m), square(m + 1))]
        return pairs[m]

    def four(m):
        if m not in fours:
            fours[m] = [a + b for a, b in zip(pair(m), pair(m + 2))]
        return fours[m]

    for j in range(count):
        shared, other = (four(j + 1), square(j)) if j % 2 == 0 else (four(j), square(j + 4))
        even, odd = [a + b for a, b in zip(shared, other)]
        both = even + odd
        up = jnp.where(top, under(first + j, 0), pltpu.roll(both, 1, 0))
        down = jnp.where(bottom, 0.0, pltpu.roll(both, 7, 0))
        even, odd = (
            both + up + jnp.where(bottom, 0.0, pltpu.roll(even, 7, 0)),
            both + down + jnp.where(top, under(first + j, 1), pltpu.roll(odd, 1, 0)),
        )
        sums = jnp.concatenate([even, odd], 0)
        high = sums.astype(B)
        parts.append(jnp.concatenate([high, (sums - high.astype(F)).astype(B)], 1))


def accumulate(nx, segments, row, moved, below, rates, masks, column_mask, start, scratch):
    kept, carry, weighted, totals = scratch
    last_slice = lax.broadcasted_iota(jnp.int32, (8, 128), 0) == 7
    carry_flat = carry.reshape(2 * nx * 4 * 16, 128)
    for slot in range(0, 8 * nx, 8):
        carry_flat[pl.ds(16 * slot + 7, 8, stride=16)] = jnp.zeros((8, 128), F)
    for x in range(nx):
        for parity in range(2):
            weighted[x, parity], totals[x, parity] = start(x, parity)
    line = lax.broadcasted_iota(jnp.int32, (256, 128), 0) % 128
    column = lax.broadcasted_iota(jnp.int32, (256, 128), 1)
    band = jnp.where(abs(line - column) <= 2, 1.0, 0.0).astype(B)
    for sy in range(5):
        place = {}
        base, todo, parts = 0, [], []
        for shift_z in range(3):
            for n, shift_x in enumerate(offsets(shift_z, sy)):
                slot = 0
                for rows in segments(shift_x, sy):
                    patch_sums(
                        rows,
                        row,
                        lambda x, parity: moved(sy, x + shift_x, shift_z, parity),
                        lambda x, parity: below(sy, x + shift_x, (shift_z - 1) * (1 + parity)) if shift_z else 0.0,
                        parts,
                    )
                    todo.append((shift_z, shift_x, rows, base, n, slot))
                    base += 16 * rows[1]
                    slot += rows[1]
        if parts:
            sums = jnp.dot(jnp.concatenate(parts, 0), band, preferred_element_type=F)
            for shift_z, shift_x, rows, at, n, slot in todo:
                for j in range(rows[1]):
                    x = rows[0] + j
                    for parity in range(2):
                        distance = sums[at + 16 * j + 8 * parity : at + 16 * j + 8 * parity + 8]
                        weight = jnp.exp2(distance * rates[parity])
                        if x < 0 or x + shift_x < 0:
                            weight = weight * masks[0]
                        if x >= nx or x + shift_x >= nx:
                            weight = weight * masks[1]
                        if column_mask is not None:
                            weight = weight * column_mask[sy]
                        spot = (sy % 2, shift_z * 5 + n, slot + j, parity)
                        kept[spot] = weight
                        place[shift_z, shift_x, x, parity] = spot
        for x in range(nx):
            gather(sy, x, place, row, moved, kept, carry.at[sy % 2, x], last_slice, weighted, totals)


def plus(a, b):
    return b if a is None else a if b is None else a + b


def gather(sy, x, place, row, moved, kept, carry, last_slice, weighted, totals):
    ahead = [[None, None], [None, None]]
    back = [[[None, None] for _ in range(3)] for _ in range(2)]
    for shift_z in range(3):
        count = [None, None]
        for shift_x in offsets(shift_z, sy):
            for parity in range(2):
                spot = place.get((shift_z, shift_x, x, parity))
                if spot is not None:
                    weight = kept[spot]
                    ahead[0][parity] = plus(ahead[0][parity], weight * moved(sy, x + shift_x, shift_z, parity))
                    count[parity] = plus(count[parity], weight)
                spot = place.get((shift_z, shift_x, x - shift_x, parity))
                if spot is not None:
                    weight = kept[spot]
                    back[0][shift_z][parity] = plus(back[0][shift_z][parity], weight * row(x - shift_x, parity))
                    back[1][shift_z][parity] = plus(back[1][shift_z][parity], weight)
        for parity in range(2):
            if shift_z + parity >= 2 and count[parity] is not None:
                count[parity] = jnp.where(last_slice, 0.0, count[parity])
            ahead[1][parity] = plus(ahead[1][parity], count[parity])
    for m, total in enumerate((weighted, totals)):
        here = [plus(back[m][0][0], None), plus(back[m][0][1], back[m][1][0])]
        for parity, up in enumerate((plus(back[m][1][1], back[m][2][0]), back[m][2][1])):
            if up is not None:
                carry[2 * m + parity, 8:16] = up
                here[parity] = plus(here[parity], carry[2 * m + parity, 7:15])
        for parity in range(2):
            term = ahead[m][parity]
            if here[parity] is not None:
                term = plus(term, lane_roll(here[parity], sy - 2))
            if term is not None:
                total[x, parity] = total[x, parity] + term


def work(nx, rows):
    return [
        pltpu.VMEM((2, 15, rows, 2, 8, 128), F),
        pltpu.VMEM((2, nx, 4, 16, 128), F),
    ]


def inner_segments(shift_x, sy):
    if sy >= SPLIT:
        return ()
    return ((2 + max(0, -shift_x), 12 - abs(shift_x)),)


def outer_segments(shift_x, sy):
    if sy >= SPLIT:
        return ((-max(0, shift_x), 16 + abs(shift_x)),)
    many = 2 + abs(shift_x)
    return ((-max(0, shift_x), many), (14 - max(0, shift_x), many))


def whole_segments(nx):
    return lambda shift_x, sy: ((-max(0, shift_x), nx + abs(shift_x)),)


def to_strips(value, chunk):
    lane = lanes() - 32 * chunk
    right = jnp.where((lane >= 16) & (lane < 24), lane_roll(value, 24 + 32 * chunk), 0.0)
    return jnp.where((lane >= 4) & (lane < 12), lane_roll(value, 4 + 32 * chunk), right)


def inner_kernel(noisy_ref, slices_ref, own_ref, rate_ref, copies, weighted, totals, rim_ref, left_ref, right_ref, steps, below, *scratch):
    def row(x, parity):
        return own_ref[x, parity]

    flat = noisy_ref.reshape(256, 128)
    for x in range(16):
        for parity in range(2):
            own_ref[x, parity] = flat[pl.ds(parity * 16 + x, 8, stride=32)]
    fill_copies(copies, steps, 16, row)
    fill_below(below, range(2, 14), row)
    lane = lanes()
    place = (lane % 32) // 4
    for x in range(12):
        for parity in range(2):
            value = jnp.zeros((8, 128), F)
            for chunk in range(4):
                source = 4 * chunk + x - HALO
                if 0 <= source < 16:
                    value = value + to_strips(own_ref[source, parity], chunk)
            rim_ref[x, parity] = value
    for group in range(3):
        for ref, column in ((left_ref, 0), (right_ref, 124)):
            message = jnp.zeros((8, 128), F)
            for chunk in range(4):
                for slot in range(8):
                    source = 4 * chunk + 4 * group + slot // 2 - HALO
                    if 0 <= source < 16:
                        here = (place == slot) & (lane // 32 == chunk)
                        message = jnp.where(here, lane_roll(own_ref[source, slot % 2], 32 * chunk + 4 * slot - column), message)
            ref[group] = message
    slices = jnp.broadcast_to(slices_ref[...], (8, 16))
    sublane, lane = [lax.broadcasted_iota(jnp.int32, (8, 16), dim) for dim in range(2)]
    for parity in range(2):
        rate = jnp.sum(jnp.where(lane == 2 * sublane + parity, slices, 0.0), axis=1, keepdims=True)
        rate_ref[parity] = jnp.broadcast_to(rate, (8, 128))

    one = jnp.ones((8, 128), F)
    accumulate(
        16,
        inner_segments,
        row,
        lambda sy, x, shift_z, parity: moved_row(copies, sy, x, shift_z, parity),
        lambda sy, x, j: below[sy, x - 2, j],
        (rate_ref[0], rate_ref[1]),
        None,
        None,
        lambda x, parity: (own_ref[x, parity], one),
        (*scratch, weighted, totals),
    )


def join_kernel(
    next_ref, pair_ref, rim_ref, left_ref, right_ref, own_ref, copies, rate_ref, inner_w, inner_t,
    low_ref, high_ref, rim_out, first_out, second_out, mid_ref, *scratch,
):
    odd = flag("odd_x") > 0.5
    pair, other = pair_ref.reshape(256, 128), next_ref.reshape(256, 128)
    for x in range(HALO):
        for parity in range(2):
            line = pl.ds(parity * 16 + 12 + x, 8, stride=32)
            low_ref[x, parity] = jnp.where(odd, pair[line], other[line])
            line = pl.ds(parity * 16 + x, 8, stride=32)
            high_ref[x, parity] = jnp.where(odd, other[line], pair[line])
    lane = lanes()
    place = (lane % 32) // 4
    for x in range(12):
        for parity in range(2):
            value = rim_ref[x, parity]
            if x < HALO:
                value = value + to_strips(low_ref[x, parity], 0)
            if x >= 8:
                value = value + to_strips(high_ref[x - 8, parity], 3)
            rim_out[x, parity] = value
    messages = []
    for ref, column in ((left_ref, 0), (right_ref, 124)):
        groups = [ref[0], ref[1], ref[2]]
        for group, halo, chunk in ((0, low_ref, 0), (2, high_ref, 3)):
            for slot in range(8):
                here = (place == slot) & (lane // 32 == chunk)
                piece = lane_roll(halo[slot // 2, slot % 2], 32 * chunk + 4 * slot - column)
                groups[group] = jnp.where(here, piece, groups[group])
        messages.append(groups)
    odd = flag("odd_y") > 0.5
    for group in range(3):
        left, right = messages[0][group], messages[1][group]
        first_out[group] = jnp.where(odd, left, right)
        second_out[group] = jnp.where(odd, right, left)

    @pl.when(starts_early())
    def _():
        outer_rows(own_ref, low_ref, high_ref, copies, rate_ref, inner_w, inner_t, mid_ref, *scratch)


def starts_early():
    return 2 * lax.axis_index("gy") < lax.axis_size("gy")


def outer_kernel(own_ref, low_ref, high_ref, copies, rate_ref, inner_w, inner_t, done_ref, mid_ref, *scratch):
    early = starts_early()

    @pl.when(early)
    def _():
        mid_ref[...] = done_ref[...]

    @pl.when(jnp.logical_not(early))
    def _():
        outer_rows(own_ref, low_ref, high_ref, copies, rate_ref, inner_w, inner_t, mid_ref, *scratch)


def outer_rows(own_ref, low_ref, high_ref, copies, rate_ref, inner_w, inner_t, mid_ref, far, steps, below, *scratch):
    def row(x, parity):
        if x < 0:
            return low_ref[x + HALO, parity]
        return own_ref[x, parity] if x < 16 else high_ref[x - 16, parity]

    def moved(sy, x, shift_z, parity):
        if 0 <= x < 16:
            return moved_row(copies, sy, x, shift_z, parity)
        return moved_row(far, sy, x + HALO if x < 0 else x - 12, shift_z, parity)

    def taken(sy, x, j):
        return below[sy, x + 2, j]

    fill_copies(far, steps, 8, lambda x, parity: row(x - HALO if x < HALO else x + 12, parity))
    fill_below(below, range(-2, 18), row)
    one = jnp.ones((8, 128), F)
    accumulate(
        16,
        outer_segments,
        row,
        moved,
        taken,
        (rate_ref[0], rate_ref[1]),
        (flag("below"), flag("above")),
        None,
        lambda x, parity: (inner_w[x, parity], inner_t[x, parity]),
        scratch,
    )
    for x in range(16):
        for parity in range(2):
            mid_ref[x, parity] = scratch[-2][x, parity] / scratch[-1][x, parity]


def rim_kernel(rim_ref, second_ref, first_ref, rate_ref, mid_ref, out_ref, rows, copies, steps, below, column_mask, *scratch):
    lane = lanes()
    spot = lane % 32
    odd = flag("odd_y") > 0.5
    sides = [(first_ref[group], second_ref[group]) for group in range(3)]
    lefts = [jnp.where(odd, a, b) for a, b in sides]
    rights = [jnp.where(odd, b, a) for a, b in sides]
    for x in range(12):
        group, slot = x // 4, (x % 4) * 2
        for parity in range(2):
            value = rim_ref[x, parity]
            value = jnp.where(spot < 4, lane_roll(lefts[group], -4 * (slot + parity)), value)
            rows[x, parity] = jnp.where((spot >= 24) & (spot < 28), lane_roll(rights[group], 24 - 4 * (slot + parity)), value)
    for sy in range(5):
        off_left = (spot < 4) | ((spot + sy - 2 < 4) & (spot < 16))
        c = spot - 16
        off_right = (c >= 8) | ((c + sy - 2 >= 8) & (c >= 0))
        column_mask[sy] = jnp.where(off_left, flag("left"), 1.0) * jnp.where(off_right, flag("right"), 1.0)

    def row(x, parity):
        return rows[x + HALO, parity]

    fill_copies(copies, steps, 12, lambda x, parity: rows[x, parity])
    fill_below(below, range(-2, 6), row)
    one = jnp.ones((8, 128), F)
    accumulate(
        4,
        whole_segments(4),
        row,
        lambda sy, x, shift_z, parity: moved_row(copies, sy, x + HALO, shift_z, parity),
        lambda sy, x, j: below[sy, x + 2, j],
        (rate_ref[0], rate_ref[1]),
        (jnp.where(lane < 32, flag("below"), 1.0), jnp.where(lane >= 96, flag("above"), 1.0)),
        column_mask,
        lambda x, parity: (rows[x + HALO, parity], one),
        scratch,
    )
    flat = out_ref.reshape(256, 128)
    for x in range(4):
        for parity in range(2):
            value = scratch[-2][x, parity] / scratch[-1][x, parity]
            for chunk in range(4):
                at = 4 * chunk + x
                edge = jnp.where(lane < 4, lane_roll(value, -32 * chunk - 4), lane_roll(value, 104 - 32 * chunk))
                flat[pl.ds(parity * 16 + at, 8, stride=32)] = jnp.where((lane < 4) | (lane >= 124), edge, mid_ref[at, parity])


def flag(what):
    gx, gy = lax.axis_index("gx"), lax.axis_index("gy")
    holds = {
        "below": gx > 0,
        "above": gx < lax.axis_size("gx") - 1,
        "left": gy > 0,
        "right": gy < lax.axis_size("gy") - 1,
        "odd_x": gx % 2 == 1,
        "odd_y": gy % 2 == 1,
    }
    return jnp.full((8, 128), jnp.where(holds[what], 1.0, 0.0), F)


def shape(*dims):
    return jax.ShapeDtypeStruct(dims, F)


def call(kernel, name, outs, scratch, mib, flops=0):
    spec = pl.BlockSpec(memory_space=pltpu.VMEM)
    return pl.pallas_call(
        kernel,
        out_shape=outs,
        out_specs=jax.tree.map(lambda _: spec, outs),
        in_specs=INPUTS[name] * [spec],
        scratch_shapes=scratch,
        compiler_params=pltpu.CompilerParams(vmem_limit_bytes=mib * 2**20),
        cost_estimate=pl.CostEstimate(flops=flops, bytes_accessed=500_000, transcendentals=0),
        name=name,
    )


INPUTS = {"inner": 2, "join": 10, "outer": 8, "rim": 5}


def swapped(value, axis, first):
    pairs = [(a, a + 1) for a in range(first, lax.axis_size(axis) - 1, 2)]
    return lax.ppermute(value, axis, pairs + [(b, a) for a, b in pairs])


def per_device(noisy, strength):
    V = pltpu.VMEM
    row4, row12, row16, three = shape(4, 2, 8, 128), shape(12, 2, 8, 128), shape(16, 2, 8, 128), shape(3, 8, 128)
    rates = ((-math.log2(math.e) / 125.0) / strength).reshape(1, 16)
    other = swapped(noisy, "gx", 1)
    pair = swapped(noisy, "gx", 0)
    own, rate, copies, inner_w, inner_t, rim, to_left, to_right = call(
        inner_kernel,
        "inner",
        (row16, shape(2, 8, 128), shape(5, 16, 5, 8, 128), row16, row16, row12, three, three),
        [V((16, 2, 16, 128), F), V((5, 12, 3, 8, 128), F)] + work(16, 16),
        20,
        60_000_000,
    )(noisy, rates)
    outer_scratch = (
        [V((5, 8, 5, 8, 128), F), V((8, 2, 16, 128), F), V((5, 20, 3, 8, 128), F)]
        + work(16, 18)
        + [V((16, 2, 8, 128), F)] * 2
    )
    low, high, rim, first, second, done = call(
        join_kernel, "join", (row4, row4, row12, three, three, row16), outer_scratch, 20
    )(other, pair, rim, to_left, to_right, own, copies, rate, inner_w, inner_t)
    second = swapped(second, "gy", 1)
    first = swapped(first, "gy", 0)
    mid = call(outer_kernel, "outer", row16, outer_scratch, 20, 40_000_000)(
        own, low, high, copies, rate, inner_w, inner_t, done
    )
    return call(
        rim_kernel,
        "rim",
        shape(16, 16, 128),
        [V((12, 2, 8, 128), F), V((5, 12, 5, 8, 128), F), V((12, 2, 16, 128), F), V((5, 8, 3, 8, 128), F), V((5, 8, 128), F)]
        + work(4, 8)
        + [V((4, 2, 8, 128), F)] * 2,
        20,
        20_000_000,
    )(rim, second, first, rate, mid)


def solution(mesh):
    placed = (P(None, "gx", "gy"), P())
    return jax.shard_map(per_device, mesh=mesh, in_specs=placed, out_specs=P(None, "gx", "gy"), check_vma=False)
```

```python
import math

import jax
import jax.numpy as jnp
from jax import lax
from jax.experimental import pallas as pl
from jax.experimental.pallas import tpu as pltpu
from jax.sharding import PartitionSpec as P

F = jnp.float32
B = jnp.bfloat16
HALO = 4
FIRST, REST = (4, 0), (1, 2, 3)
SPLIT = 4


def lanes():
    return lax.broadcasted_iota(jnp.int32, (8, 128), 1)


def lane_roll(value, steps):
    steps %= 128
    return pltpu.roll(value, steps, 1) if steps else value


def offsets(shift_z, sy):
    if shift_z:
        return (-2, -1, 0, 1, 2)
    return (0, 1, 2) if sy > 2 else (1, 2)


def moved_row(copies, sy, row, shift_z, parity):
    return copies[sy, row, shift_z + parity]


def fill_copies(copies, steps, count, row):
    flat = steps.reshape(2 * count * 16, 128)
    for slot in range(0, 2 * count, 8):
        flat[pl.ds(16 * slot + 8, 8, stride=16)] = jnp.zeros((8, 128), F)
    for x in range(count):
        for parity in range(2):
            value = row(x, parity)
            steps[x, parity, 0:8] = value
            up = steps[x, parity, 1:9]
            for sy in range(5):
                copies[sy, x, parity] = lane_roll(value, 2 - sy)
                copies[sy, x, parity + 2] = lane_roll(up, 2 - sy)


def fill_below(below, centers, row):
    squares = {}

    def square(x):
        if x not in squares:
            squares[x] = [row(x, parity) * row(x, parity) for parity in range(2)]
        return squares[x]

    for place, x in enumerate(centers):
        sums = []
        for parity in range(2):
            near = square(x - 1)[parity] + square(x + 1)[parity]
            far = square(x - 2)[parity] + square(x + 2)[parity]
            sums.append(square(x)[parity] + near + far)
        three = (sums[0], sums[0] + sums[1], sums[1])
        for j in range(3):
            for sy in range(5):
                below[sy, place, j] = lane_roll(three[j], 2 - sy)


def patch_sums(rows, row, moved, under, parts):
    first, count = rows
    sub = lax.broadcasted_iota(jnp.int32, (8, 128), 0)
    top, bottom = sub == 0, sub == 7
    squared, pairs, fours = {}, {}, {}

    def square(m):
        if m not in squared:
            x = first - 2 + m
            differences = [row(x, parity) - moved(x, parity) for parity in range(2)]
            squared[m] = [d * d for d in differences]
        return squared[m]

    def pair(m):
        if m not in pairs:
            pairs[m] = [a + b for a, b in zip(square(m), square(m + 1))]
        return pairs[m]

    def four(m):
        if m not in fours:
            fours[m] = [a + b for a, b in zip(pair(m), pair(m + 2))]
        return fours[m]

    for j in range(count):
        shared, other = (four(j + 1), square(j)) if j % 2 == 0 else (four(j), square(j + 4))
        even, odd = [a + b for a, b in zip(shared, other)]
        both = even + odd
        up = jnp.where(top, under(first + j, 0), pltpu.roll(both, 1, 0))
        down = jnp.where(bottom, 0.0, pltpu.roll(both, 7, 0))
        even, odd = (
            both + up + jnp.where(bottom, 0.0, pltpu.roll(even, 7, 0)),
            both + down + jnp.where(top, under(first + j, 1), pltpu.roll(odd, 1, 0)),
        )
        sums = jnp.concatenate([even, odd], 0)
        high = sums.astype(B)
        parts.append(jnp.concatenate([high, (sums - high.astype(F)).astype(B)], 1))


def accumulate(nx, segments, row, moved, below, rates, masks, column_mask, start, scratch, shifts=range(5)):
    kept, carry, weighted, totals = scratch
    last_slice = lax.broadcasted_iota(jnp.int32, (8, 128), 0) == 7
    carry_flat = carry.reshape(2 * nx * 4 * 16, 128)
    for slot in range(0, 8 * nx, 8):
        carry_flat[pl.ds(16 * slot + 7, 8, stride=16)] = jnp.zeros((8, 128), F)
    for x in range(nx):
        for parity in range(2):
            weighted[x, parity], totals[x, parity] = start(x, parity)
    line = lax.broadcasted_iota(jnp.int32, (256, 128), 0) % 128
    column = lax.broadcasted_iota(jnp.int32, (256, 128), 1)
    band = jnp.where(abs(line - column) <= 2, 1.0, 0.0).astype(B)
    for sy in shifts:
        place = {}
        base, todo, parts = 0, [], []
        for shift_z in range(3):
            for n, shift_x in enumerate(offsets(shift_z, sy)):
                slot = 0
                for rows in segments(shift_x, sy):
                    patch_sums(
                        rows,
                        row,
                        lambda x, parity: moved(sy, x + shift_x, shift_z, parity),
                        lambda x, parity: below(sy, x + shift_x, (shift_z - 1) * (1 + parity)) if shift_z else 0.0,
                        parts,
                    )
                    todo.append((shift_z, shift_x, rows, base, n, slot))
                    base += 16 * rows[1]
                    slot += rows[1]
        if parts:
            sums = jnp.dot(jnp.concatenate(parts, 0), band, preferred_element_type=F)
            for shift_z, shift_x, rows, at, n, slot in todo:
                for j in range(rows[1]):
                    x = rows[0] + j
                    for parity in range(2):
                        distance = sums[at + 16 * j + 8 * parity : at + 16 * j + 8 * parity + 8]
                        weight = jnp.exp2(distance * rates[parity])
                        if x < 0 or x + shift_x < 0:
                            weight = weight * masks[0]
                        if x >= nx or x + shift_x >= nx:
                            weight = weight * masks[1]
                        if column_mask is not None:
                            weight = weight * column_mask[sy]
                        spot = (sy % 2, shift_z * 5 + n, slot + j, parity)
                        kept[spot] = weight
                        place[shift_z, shift_x, x, parity] = spot
        for x in range(nx):
            gather(sy, x, place, row, moved, kept, carry.at[sy % 2, x], last_slice, weighted, totals)


def plus(a, b):
    return b if a is None else a if b is None else a + b


def gather(sy, x, place, row, moved, kept, carry, last_slice, weighted, totals):
    ahead = [[None, None], [None, None]]
    back = [[[None, None] for _ in range(3)] for _ in range(2)]
    for shift_z in range(3):
        count = [None, None]
        for shift_x in offsets(shift_z, sy):
            for parity in range(2):
                spot = place.get((shift_z, shift_x, x, parity))
                if spot is not None:
                    weight = kept[spot]
                    ahead[0][parity] = plus(ahead[0][parity], weight * moved(sy, x + shift_x, shift_z, parity))
                    count[parity] = plus(count[parity], weight)
                spot = place.get((shift_z, shift_x, x - shift_x, parity))
                if spot is not None:
                    weight = kept[spot]
                    back[0][shift_z][parity] = plus(back[0][shift_z][parity], weight * row(x - shift_x, parity))
                    back[1][shift_z][parity] = plus(back[1][shift_z][parity], weight)
        for parity in range(2):
            if shift_z + parity >= 2 and count[parity] is not None:
                count[parity] = jnp.where(last_slice, 0.0, count[parity])
            ahead[1][parity] = plus(ahead[1][parity], count[parity])
    for m, total in enumerate((weighted, totals)):
        here = [plus(back[m][0][0], None), plus(back[m][0][1], back[m][1][0])]
        for parity, up in enumerate((plus(back[m][1][1], back[m][2][0]), back[m][2][1])):
            if up is not None:
                carry[2 * m + parity, 8:16] = up
                here[parity] = plus(here[parity], carry[2 * m + parity, 7:15])
        for parity in range(2):
            term = ahead[m][parity]
            if here[parity] is not None:
                term = plus(term, lane_roll(here[parity], sy - 2))
            if term is not None:
                total[x, parity] = total[x, parity] + term


def work(nx, rows):
    return [
        pltpu.VMEM((2, 15, rows, 2, 8, 128), F),
        pltpu.VMEM((2, nx, 4, 16, 128), F),
    ]


def inner_segments(shift_x, sy):
    if sy >= SPLIT:
        return ()
    return ((2 + max(0, -shift_x), 12 - abs(shift_x)),)


def outer_segments(shift_x, sy):
    if sy >= SPLIT:
        return ((-max(0, shift_x), 16 + abs(shift_x)),)
    many = 2 + abs(shift_x)
    return ((-max(0, shift_x), many), (14 - max(0, shift_x), many))


def whole_segments(nx):
    return lambda shift_x, sy: ((-max(0, shift_x), nx + abs(shift_x)),)


def to_strips(value, chunk):
    lane = lanes() - 32 * chunk
    right = jnp.where((lane >= 16) & (lane < 24), lane_roll(value, 24 + 32 * chunk), 0.0)
    return jnp.where((lane >= 4) & (lane < 12), lane_roll(value, 4 + 32 * chunk), right)


def inner_kernel(noisy_ref, slices_ref, own_ref, rate_ref, copies, weighted, totals, rim_ref, left_ref, right_ref, steps, below, *scratch):
    def row(x, parity):
        return own_ref[x, parity]

    flat = noisy_ref.reshape(256, 128)
    for x in range(16):
        for parity in range(2):
            own_ref[x, parity] = flat[pl.ds(parity * 16 + x, 8, stride=32)]
    fill_copies(copies, steps, 16, row)
    fill_below(below, range(2, 14), row)
    lane = lanes()
    place = (lane % 32) // 4
    for x in range(12):
        for parity in range(2):
            value = jnp.zeros((8, 128), F)
            for chunk in range(4):
                source = 4 * chunk + x - HALO
                if 0 <= source < 16:
                    value = value + to_strips(own_ref[source, parity], chunk)
            rim_ref[x, parity] = value
    for group in range(3):
        for ref, column in ((left_ref, 0), (right_ref, 124)):
            message = jnp.zeros((8, 128), F)
            for chunk in range(4):
                for slot in range(8):
                    source = 4 * chunk + 4 * group + slot // 2 - HALO
                    if 0 <= source < 16:
                        here = (place == slot) & (lane // 32 == chunk)
                        message = jnp.where(here, lane_roll(own_ref[source, slot % 2], 32 * chunk + 4 * slot - column), message)
            ref[group] = message
    slices = jnp.broadcast_to(slices_ref[...], (8, 16))
    sublane, lane = [lax.broadcasted_iota(jnp.int32, (8, 16), dim) for dim in range(2)]
    for parity in range(2):
        rate = jnp.sum(jnp.where(lane == 2 * sublane + parity, slices, 0.0), axis=1, keepdims=True)
        rate_ref[parity] = jnp.broadcast_to(rate, (8, 128))

    one = jnp.ones((8, 128), F)
    accumulate(
        16,
        inner_segments,
        row,
        lambda sy, x, shift_z, parity: moved_row(copies, sy, x, shift_z, parity),
        lambda sy, x, j: below[sy, x - 2, j],
        (rate_ref[0], rate_ref[1]),
        None,
        None,
        lambda x, parity: (own_ref[x, parity], one),
        (*scratch, weighted, totals),
    )


def join_kernel(
    next_ref, pair_ref, rim_ref, left_ref, right_ref, own_ref, copies, rate_ref, inner_w, inner_t,
    low_ref, high_ref, rim_out, first_out, second_out, sum_w, sum_t, *scratch,
):
    odd = flag("odd_x") > 0.5
    pair, other = pair_ref.reshape(256, 128), next_ref.reshape(256, 128)
    for x in range(HALO):
        for parity in range(2):
            line = pl.ds(parity * 16 + 12 + x, 8, stride=32)
            low_ref[x, parity] = jnp.where(odd, pair[line], other[line])
            line = pl.ds(parity * 16 + x, 8, stride=32)
            high_ref[x, parity] = jnp.where(odd, other[line], pair[line])
    lane = lanes()
    place = (lane % 32) // 4
    for x in range(12):
        for parity in range(2):
            value = rim_ref[x, parity]
            if x < HALO:
                value = value + to_strips(low_ref[x, parity], 0)
            if x >= 8:
                value = value + to_strips(high_ref[x - 8, parity], 3)
            rim_out[x, parity] = value
    messages = []
    for ref, column in ((left_ref, 0), (right_ref, 124)):
        groups = [ref[0], ref[1], ref[2]]
        for group, halo, chunk in ((0, low_ref, 0), (2, high_ref, 3)):
            for slot in range(8):
                here = (place == slot) & (lane // 32 == chunk)
                piece = lane_roll(halo[slot // 2, slot % 2], 32 * chunk + 4 * slot - column)
                groups[group] = jnp.where(here, piece, groups[group])
        messages.append(groups)
    odd = flag("odd_y") > 0.5
    for group in range(3):
        left, right = messages[0][group], messages[1][group]
        first_out[group] = jnp.where(odd, left, right)
        second_out[group] = jnp.where(odd, right, left)

    @pl.when(starts_early())
    def _():
        outer_rows(own_ref, low_ref, high_ref, copies, rate_ref, inner_w, inner_t, FIRST, sum_w, sum_t, *scratch)


def starts_early():
    return 2 * lax.axis_index("gy") < lax.axis_size("gy")


def outer_kernel(own_ref, low_ref, high_ref, copies, rate_ref, inner_w, inner_t, done_w, done_t, mid_ref, sum_w, sum_t, *scratch):
    early = starts_early()

    @pl.when(early)
    def _():
        sum_w[...] = done_w[...]
        sum_t[...] = done_t[...]

    @pl.when(jnp.logical_not(early))
    def _():
        outer_rows(own_ref, low_ref, high_ref, copies, rate_ref, inner_w, inner_t, FIRST, sum_w, sum_t, *scratch)

    outer_rows(own_ref, low_ref, high_ref, copies, rate_ref, sum_w, sum_t, REST, sum_w, sum_t, *scratch)
    for x in range(16):
        for parity in range(2):
            mid_ref[x, parity] = sum_w[x, parity] / sum_t[x, parity]


def outer_rows(own_ref, low_ref, high_ref, copies, rate_ref, from_w, from_t, shifts, sum_w, sum_t, far, steps, below, *scratch):
    def row(x, parity):
        if x < 0:
            return low_ref[x + HALO, parity]
        return own_ref[x, parity] if x < 16 else high_ref[x - 16, parity]

    def moved(sy, x, shift_z, parity):
        if 0 <= x < 16:
            return moved_row(copies, sy, x, shift_z, parity)
        return moved_row(far, sy, x + HALO if x < 0 else x - 12, shift_z, parity)

    def taken(sy, x, j):
        return below[sy, x + 2, j]

    fill_copies(far, steps, 8, lambda x, parity: row(x - HALO if x < HALO else x + 12, parity))
    fill_below(below, range(-2, 18), row)
    one = jnp.ones((8, 128), F)
    accumulate(
        16,
        outer_segments,
        row,
        moved,
        taken,
        (rate_ref[0], rate_ref[1]),
        (flag("below"), flag("above")),
        None,
        lambda x, parity: (from_w[x, parity], from_t[x, parity]),
        (*scratch, sum_w, sum_t),
        shifts,
    )


def rim_kernel(rim_ref, second_ref, first_ref, rate_ref, mid_ref, out_ref, rows, copies, steps, below, column_mask, *scratch):
    lane = lanes()
    spot = lane % 32
    odd = flag("odd_y") > 0.5
    sides = [(first_ref[group], second_ref[group]) for group in range(3)]
    lefts = [jnp.where(odd, a, b) for a, b in sides]
    rights = [jnp.where(odd, b, a) for a, b in sides]
    for x in range(12):
        group, slot = x // 4, (x % 4) * 2
        for parity in range(2):
            value = rim_ref[x, parity]
            value = jnp.where(spot < 4, lane_roll(lefts[group], -4 * (slot + parity)), value)
            rows[x, parity] = jnp.where((spot >= 24) & (spot < 28), lane_roll(rights[group], 24 - 4 * (slot + parity)), value)
    for sy in range(5):
        off_left = (spot < 4) | ((spot + sy - 2 < 4) & (spot < 16))
        c = spot - 16
        off_right = (c >= 8) | ((c + sy - 2 >= 8) & (c >= 0))
        column_mask[sy] = jnp.where(off_left, flag("left"), 1.0) * jnp.where(off_right, flag("right"), 1.0)

    def row(x, parity):
        return rows[x + HALO, parity]

    fill_copies(copies, steps, 12, lambda x, parity: rows[x, parity])
    fill_below(below, range(-2, 6), row)
    one = jnp.ones((8, 128), F)
    accumulate(
        4,
        whole_segments(4),
        row,
        lambda sy, x, shift_z, parity: moved_row(copies, sy, x + HALO, shift_z, parity),
        lambda sy, x, j: below[sy, x + 2, j],
        (rate_ref[0], rate_ref[1]),
        (jnp.where(lane < 32, flag("below"), 1.0), jnp.where(lane >= 96, flag("above"), 1.0)),
        column_mask,
        lambda x, parity: (rows[x + HALO, parity], one),
        scratch,
    )
    flat = out_ref.reshape(256, 128)
    for x in range(4):
        for parity in range(2):
            value = scratch[-2][x, parity] / scratch[-1][x, parity]
            for chunk in range(4):
                at = 4 * chunk + x
                edge = jnp.where(lane < 4, lane_roll(value, -32 * chunk - 4), lane_roll(value, 104 - 32 * chunk))
                flat[pl.ds(parity * 16 + at, 8, stride=32)] = jnp.where((lane < 4) | (lane >= 124), edge, mid_ref[at, parity])


def flag(what):
    gx, gy = lax.axis_index("gx"), lax.axis_index("gy")
    holds = {
        "below": gx > 0,
        "above": gx < lax.axis_size("gx") - 1,
        "left": gy > 0,
        "right": gy < lax.axis_size("gy") - 1,
        "odd_x": gx % 2 == 1,
        "odd_y": gy % 2 == 1,
    }
    return jnp.full((8, 128), jnp.where(holds[what], 1.0, 0.0), F)


def shape(*dims):
    return jax.ShapeDtypeStruct(dims, F)


def call(kernel, name, outs, scratch, mib, flops=0):
    spec = pl.BlockSpec(memory_space=pltpu.VMEM)
    return pl.pallas_call(
        kernel,
        out_shape=outs,
        out_specs=jax.tree.map(lambda _: spec, outs),
        in_specs=INPUTS[name] * [spec],
        scratch_shapes=scratch,
        compiler_params=pltpu.CompilerParams(vmem_limit_bytes=mib * 2**20),
        cost_estimate=pl.CostEstimate(flops=flops, bytes_accessed=500_000, transcendentals=0),
        name=name,
    )


INPUTS = {"inner": 2, "join": 10, "outer": 9, "rim": 5}


def swapped(value, axis, first):
    pairs = [(a, a + 1) for a in range(first, lax.axis_size(axis) - 1, 2)]
    return lax.ppermute(value, axis, pairs + [(b, a) for a, b in pairs])


def per_device(noisy, strength):
    V = pltpu.VMEM
    row4, row12, row16, three = shape(4, 2, 8, 128), shape(12, 2, 8, 128), shape(16, 2, 8, 128), shape(3, 8, 128)
    rates = ((-math.log2(math.e) / 125.0) / strength).reshape(1, 16)
    other = swapped(noisy, "gx", 1)
    pair = swapped(noisy, "gx", 0)
    own, rate, copies, inner_w, inner_t, rim, to_left, to_right = call(
        inner_kernel,
        "inner",
        (row16, shape(2, 8, 128), shape(5, 16, 5, 8, 128), row16, row16, row12, three, three),
        [V((16, 2, 16, 128), F), V((5, 12, 3, 8, 128), F)] + work(16, 16),
        20,
        60_000_000,
    )(noisy, rates)
    outer_scratch = (
        [V((5, 8, 5, 8, 128), F), V((8, 2, 16, 128), F), V((5, 20, 3, 8, 128), F)]
        + work(16, 18)
    )
    low, high, rim, first, second, done_w, done_t = call(
        join_kernel, "join", (row4, row4, row12, three, three, row16, row16), outer_scratch, 20
    )(other, pair, rim, to_left, to_right, own, copies, rate, inner_w, inner_t)
    second = swapped(second, "gy", 1)
    first = swapped(first, "gy", 0)
    mid = call(outer_kernel, "outer", row16, [V((16, 2, 8, 128), F)] * 2 + outer_scratch, 20, 40_000_000)(
        own, low, high, copies, rate, inner_w, inner_t, done_w, done_t
    )
    return call(
        rim_kernel,
        "rim",
        shape(16, 16, 128),
        [V((12, 2, 8, 128), F), V((5, 12, 5, 8, 128), F), V((12, 2, 16, 128), F), V((5, 8, 3, 8, 128), F), V((5, 8, 128), F)]
        + work(4, 8)
        + [V((4, 2, 8, 128), F)] * 2,
        20,
        20_000_000,
    )(rim, second, first, rate, mid)


def solution(mesh):
    placed = (P(None, "gx", "gy"), P())
    return jax.shard_map(per_device, mesh=mesh, in_specs=placed, out_specs=P(None, "gx", "gy"), check_vma=False)
```
